32 devices in a mesh: takers: 16 (over z, y, x), nodes: 2 (over core).
Axes of the slice: x: 2, y: 2, z: 4, core: 2. Of those that a mesh axis runs over, the one named last changes fastest.
Arguments:
- slopes: bfloat16 [3, 65536], P(None, 'takers'), may hold values from 0.29882812 to 1.5
- intercepts: bfloat16 [65536], P('takers'), may hold values from -3 to 3
- guessing: bfloat16 [65536], P('takers'), may hold values from 0.049804688 to 0.29882812
- responses: int32 [64, 12, 128, 128], P('takers'), may hold values from 0 to 2, as said below
- tile_items: int32 [64, 12], P('takers'), may hold values from 0 to 511, as said below
- tile_count: int32 [64], P('takers'), may hold values from 4 to 12, as said below
Outputs:
- new_params: float32 [4, 65536], P(None, 'takers')
- marginal: float32 [8192], P('takers')
- posterior_mean: float32 [3, 8192], P(None, 'takers')
The draws below stay inside these ranges and needn't reach their ends.
Inputs may be any that keep to these rules, and one draw needn't show every extreme that they name: `tile_items`: within a row block the used slots name distinct item blocks; some row block uses all 12 slots. `tile_count`: some row block uses all 12 slots; slots at or beyond the count are ignored. `responses`: 0 means not answered, 1 a wrong answer, 2 a right answer; most entries are 0.
All inputs are finite; a program needn't handle non-finite values.
Results may differ from the reference program's by a relative error of at most 0.0041.
Values may be sent and summed in bfloat16 or wider, within the bound.
A program may use at most 64 MiB of HBM per device.

```python
import math
import jax
import jax.numpy as jnp
from jax import lax

ITEMS = 65536
TILE = 128
NODES_1D = 16
KT = 12
NODES = 4096
TAKERS = 8192
ROWBLK = 64
BLOCKS = 512


def draw_tile_items(key, part):
    row_keys = jax.random.split(jax.random.fold_in(key, 11), ROWBLK)
    return jax.vmap(lambda row_key: jax.random.permutation(row_key, ITEMS // TILE)[:KT])(row_keys).astype(jnp.int32)


def draw_tile_count(key, part):
    counts = jax.random.randint(jax.random.fold_in(key, 23), (ROWBLK,), max(1, KT // 3), KT + 1, dtype=jnp.int32)
    full_row = jax.random.randint(jax.random.fold_in(key, 29), (), 0, ROWBLK, dtype=jnp.int32)
    return counts.at[full_row].set(KT)


def draw_responses(key, part):
    shape = (ROWBLK, KT, TILE, TILE)
    seen = jax.random.randint(jax.random.fold_in(key, 31), shape, 0, 8, dtype=jnp.int32) == 0
    dense_taker = jax.random.randint(jax.random.fold_in(key, 41), (ROWBLK, 1, TILE, 1), 0, 16, dtype=jnp.int32) == 0
    seen = jnp.logical_or(seen, dense_taker)
    right_bit = jax.random.randint(jax.random.fold_in(key, 37), shape, 0, 2, dtype=jnp.int32)
    codes = jnp.where(seen, 1 + right_bit, 0).astype(jnp.int32)
    return codes.at[0, 0, 0, 0].set(2).at[0, 0, 0, 1].set(1)


def steps_of(key, extent, shards, low, largest):
    factor_of = 1.0
    for position, shards_of in shards:
        draws = jax.random.uniform(jax.random.fold_in(jax.random.fold_in(key, 6), position), (shards_of,), jnp.float32, low / len(shards), largest / len(shards))
        factor_of = factor_of * jnp.repeat(jnp.exp(draws), extent[position] // shards_of).reshape((-1,) + (1,) * (len(extent) - 1 - position))
    return factor_of


def scatter_about(own_key, extent, width, most, pieces=(), kind=jnp.bfloat16):
    loudness = steps_of(own_key, extent, pieces, -0.22, 0.18) if pieces else 1.0
    values = jax.random.normal(own_key, extent, jnp.float32) * width * loudness
    return jnp.minimum(jnp.maximum(values, -most), most).astype(kind)


def setup_inputs(seed: int = 0) -> dict:
    keys = jax.random.split(jax.random.key(seed), 7)
    slopes = jnp.clip(jnp.exp(math.log(1.5) - 1.6133518 * jax.random.uniform(keys[0], (3, ITEMS), jnp.float32) ** steps_of(keys[0], (3, ITEMS), ((1, 16),), -0.2, 0.2)), 0.29882812, 1.5).astype(jnp.bfloat16)
    intercepts = scatter_about(keys[1], (ITEMS,), 1.0, 3.0, ((0, 16),))
    guessing = jnp.clip(0.049804688 + 0.24902344 * jax.random.uniform(keys[2], (ITEMS,), jnp.float32) ** steps_of(keys[2], (ITEMS,), ((0, 16),), -0.2, 0.2), 0.049804688, 0.29882812).astype(jnp.bfloat16)
    responses = draw_responses(jax.random.fold_in(keys[6], 71), 0)
    tile_items = draw_tile_items(jax.random.fold_in(keys[6], 71), 0)
    tile_count = draw_tile_count(jax.random.fold_in(keys[6], 71), 0)
    return dict(slopes=slopes, intercepts=intercepts, guessing=guessing, responses=responses, tile_items=tile_items, tile_count=tile_count)


def node_grid(first_node, how_many, grid_side):
    node_index = first_node + jnp.arange(how_many, dtype=jnp.int32)
    lattice = jnp.stack([node_index // (grid_side * grid_side), (node_index // grid_side) % grid_side, node_index % grid_side]).astype(jnp.float32)
    return -3.0 + 6.0 * lattice / (grid_side - 1)


def log_prior(node_points, grid_side):
    whole = node_grid(0, grid_side ** 3, grid_side)
    log_total = jnp.log(jnp.sum(jnp.exp(-0.5 * jnp.sum(whole * whole, axis=0))))
    return -0.5 * jnp.sum(node_points * node_points, axis=0) - log_total


def tile_logits(slope_blk, icpt_blk, node_points):
    return (slope_blk[:, 0, :, None] * node_points[0] + slope_blk[:, 1, :, None] * node_points[1]
            + slope_blk[:, 2, :, None] * node_points[2] + icpt_blk[:, :, None])


def reference(slopes, intercepts, guessing, responses, tile_items, tile_count):
    grid_side = NODES_1D
    node_points = node_grid(0, NODES, grid_side)
    prior_here = log_prior(node_points, grid_side)
    slope_tab = slopes.astype(jnp.float32).reshape(3, BLOCKS, TILE)
    icpt_tab = intercepts.astype(jnp.float32).reshape(BLOCKS, TILE)
    guess_tab = guessing.astype(jnp.float32).reshape(BLOCKS, TILE)
    features = jnp.concatenate([node_points, jnp.ones((1, NODES), jnp.float32)], axis=0)

    def per_block(inputs):
        answers, block_ids, filled = inputs
        live_mask = (jnp.arange(KT, dtype=jnp.int32) < filled).astype(jnp.float32)[:, None, None]
        slope_blk = jnp.transpose(slope_tab[:, block_ids], (1, 0, 2))
        logits = tile_logits(slope_blk, icpt_tab[block_ids], node_points)
        guess_rate = guess_tab[block_ids][:, :, None]
        sig_pos = jax.nn.sigmoid(logits)
        sig_neg = jax.nn.sigmoid(-logits)
        correct = guess_rate + (1.0 - guess_rate) * sig_pos
        log_miss = jnp.log(1.0 - guess_rate) + jax.nn.log_sigmoid(-logits)
        log_right = (jnp.log(correct) * live_mask).astype(jnp.bfloat16)
        log_wrong = (log_miss * live_mask).astype(jnp.bfloat16)
        right_f = (answers == 2).astype(jnp.float32)
        wrong_f = (answers == 1).astype(jnp.float32)
        answered_f = right_f + wrong_f
        loglik = (jnp.einsum('kti,kiq->tq', right_f, log_right.astype(jnp.float32))
                  + jnp.einsum('kti,kiq->tq', wrong_f, log_wrong.astype(jnp.float32)) + prior_here)
        row_max = jnp.max(loglik, axis=1)
        weights = jnp.exp(loglik - row_max[:, None])
        row_mass = jnp.sum(weights, axis=1)
        moment = jnp.einsum('cq,tq->ct', node_points, weights, precision=lax.Precision.HIGHEST)
        log_norm = row_max + jnp.log(row_mass)
        mean_here = moment / row_mass
        posterior = jnp.exp(loglik - log_norm[:, None]).astype(jnp.bfloat16)
        post_f = posterior.astype(jnp.float32)
        correct_mass = jnp.einsum('kti,tq->kiq', right_f, post_f)
        node_mass = jnp.einsum('kti,tq->kiq', answered_f, post_f)
        gradient = (correct_mass - node_mass * correct) * (sig_pos / correct) * live_mask
        fisher = node_mass * (1.0 - guess_rate) * sig_pos * sig_pos * sig_neg / correct * live_mask
        grad_terms = jnp.einsum('kiq,cq->kci', gradient, features, precision=lax.Precision.HIGHEST)
        fisher_terms = jnp.einsum('kiq,cq->kci', fisher, features * features, precision=lax.Precision.HIGHEST)
        return log_norm, mean_here, jnp.concatenate([grad_terms, fisher_terms], axis=1)

    log_norms, means, tile_stats = lax.map(per_block, (responses, tile_items, tile_count))
    marginal = log_norms.reshape(TAKERS)
    posterior_mean = jnp.transpose(means, (1, 0, 2)).reshape(3, TAKERS)
    flat_stats = jnp.transpose(tile_stats, (2, 0, 1, 3)).reshape(8, ROWBLK * KT, TILE)
    item_totals = jnp.zeros((8, BLOCKS, TILE), jnp.float32).at[:, tile_items.reshape(-1)].add(flat_stats)
    item_totals = item_totals.reshape(8, ITEMS)
    current = jnp.concatenate([slopes.astype(jnp.float32), intercepts.astype(jnp.float32)[None]], axis=0)
    new_params = current + item_totals[:4] / (item_totals[4:] + 1.0)
    return new_params, marginal, posterior_mean
```

```python
import functools

import jax
import jax.numpy as jnp
from jax import lax
from jax.experimental import pallas as pl
from jax.experimental.pallas import tpu as pltpu
from jax.sharding import PartitionSpec as P

SIDE = 16
STEP = 6.0 / (SIDE - 1)
VMEM_LIMIT = 56 * 1024 * 1024


def lattice_point(index):
    return -3.0 + 6.0 * index.astype(jnp.float32) / (SIDE - 1)


def item_rows(tab_ref, block):
    return [tab_ref[p, pl.ds(block, 1), :] for p in range(5)]


def exp_factors(rows, x0, planes, ey_ref, w_ref):
    a0, a1, a2, d, _ = rows
    line = lattice_point(lax.broadcasted_iota(jnp.int32, (SIDE, a0.shape[1]), 0))
    ey_ref[...] = jnp.exp(a1 * line)
    ez = jnp.exp(a2 * line + d)
    ex = jnp.exp(a0 * lattice_point(x0 + lax.broadcasted_iota(jnp.int32, (SIDE, a0.shape[1]), 0)))
    for x in range(planes):
        w_ref[x * SIDE:(x + 1) * SIDE, :] = ez * ex[x:x + 1, :]


def row_index(shape):
    return lax.broadcasted_iota(jnp.int32, shape, 0)


def loglik_kernel(planes, items_ref, count_ref, x0_ref, resp_ref, tab_ref, ll_ref, red_ref, ey_ref, w_ref):
    b = pl.program_id(0)
    x0 = x0_ref[0]
    rows_y = planes * SIDE
    lanes = resp_ref.shape[-1]
    line = lattice_point(row_index((SIDE, lanes)))
    log_total = 3.0 * jnp.log(jnp.sum(jnp.exp(-0.5 * line * line), axis=0, keepdims=True))
    within = row_index((rows_y, lanes))
    th0 = lattice_point(x0 + within // SIDE)
    th2 = lattice_point(within % SIDE)
    prior_xz = -0.5 * (th0 * th0 + th2 * th2) - log_total

    def init(y, carry):
        th1 = lattice_point(jnp.full((1, lanes), y, jnp.int32))
        ll_ref[0, pl.ds(pl.multiple_of(y * rows_y, rows_y), rows_y), :] = prior_xz - 0.5 * th1 * th1
        return carry

    lax.fori_loop(0, SIDE, init, 0)

    def slot(k, carry):
        rows = item_rows(tab_ref, items_ref[b, k])
        exp_factors(rows, x0, planes, ey_ref, w_ref)
        guess = rows[4]
        log_rest = jnp.log(1.0 - guess)
        codes = resp_ref[0, k]
        ind = jnp.concatenate([(codes == 2).astype(jnp.bfloat16), (codes == 1).astype(jnp.bfloat16)], axis=1)

        def chunk(y, carry):
            u = w_ref[...] * ey_ref[pl.ds(y, 1), :]
            log_all = jnp.log(1.0 + u)
            log_right = jnp.log(guess + u) - log_all
            log_wrong = log_rest - log_all
            table = jnp.concatenate([log_right.astype(jnp.bfloat16), log_wrong.astype(jnp.bfloat16)], axis=1)
            part = lax.dot_general(table, ind, (((1,), (1,)), ((), ())), preferred_element_type=jnp.float32)
            ll_ref[0, pl.ds(pl.multiple_of(y * rows_y, rows_y), rows_y), :] += part
            return carry

        return lax.fori_loop(0, SIDE, chunk, carry, unroll=4)

    lax.fori_loop(0, count_ref[b], slot, 0)

    row_max = jnp.max(ll_ref[0], axis=0, keepdims=True)
    zero = jnp.zeros((rows_y, lanes), jnp.float32)

    def weigh(y, carry):
        total, by_y = carry
        w = jnp.exp(ll_ref[0, pl.ds(pl.multiple_of(y * rows_y, rows_y), rows_y), :] - row_max)
        th1 = lattice_point(jnp.full((1, lanes), y, jnp.int32))
        return total + w, by_y + w * th1

    total, by_y = lax.fori_loop(0, SIDE, weigh, (zero, zero))
    sums = [total, total * th0, by_y, total * th2]
    red_ref[0] = jnp.concatenate(
        [row_max] + [jnp.sum(s, axis=0, keepdims=True) for s in sums] + [jnp.zeros((3, lanes), jnp.float32)], axis=0)


def stats_kernel(planes, items_ref, count_ref, x0_ref, resp_ref, tab_ref, ll_ref, norm_ref, out_ref, ey_ref, w_ref, post_ref):
    b = pl.program_id(0)
    x0 = x0_ref[0]
    rows_y = planes * SIDE
    lanes = resp_ref.shape[-1]

    @pl.when(b == 0)
    def _():
        out_ref[...] = jnp.zeros_like(out_ref)

    log_norm = norm_ref[0, 0:1, :]
    post_ref[...] = jnp.exp(ll_ref[0] - log_norm).astype(jnp.bfloat16)
    th2 = lattice_point(row_index((SIDE, lanes)))

    def slot(k, carry):
        block = items_ref[b, k]
        rows = item_rows(tab_ref, block)
        exp_factors(rows, x0, planes, ey_ref, w_ref)
        guess = rows[4]
        codes = resp_ref[0, k]
        ind = jnp.concatenate([(codes == 2).astype(jnp.bfloat16), (codes > 0).astype(jnp.bfloat16)], axis=1)
        zero = jnp.zeros((SIDE, lanes), jnp.float32)

        def chunk(y, sums):
            post = post_ref[pl.ds(pl.multiple_of(y * rows_y, rows_y), rows_y), :]
            both = jnp.dot(post, ind, preferred_element_type=jnp.float32)
            e1 = ey_ref[pl.ds(y, 1), :]
            th1 = lattice_point(jnp.full((1, lanes), y, jnp.int32))
            s0 = s1 = f0 = f1 = zero
            for x in range(planes):
                lo, hi = x * SIDE, (x + 1) * SIDE
                hits, mass = both[lo:hi, :lanes], both[lo:hi, lanes:]
                u = w_ref[lo:hi, :] * e1
                cu, u1 = guess + u, 1.0 + u
                uk = u * pl.reciprocal(cu * u1)
                mc = mass * cu
                score = (hits * u1 - mc) * uk
                fisher = mc * (uk * uk)
                th0 = -3.0 + STEP * (x0 + x).astype(jnp.float32)
                s0, f0 = s0 + score, f0 + fisher
                s1, f1 = s1 + score * th0, f1 + fisher * (th0 * th0)
            g, gy, gx, h, hy, hx = sums
            return g + s0, gy + s0 * th1, gx + s1, h + f0, hy + f0 * (th1 * th1), hx + f1

        g, gy, gx, h, hy, hx = lax.fori_loop(0, SIDE, chunk, (zero,) * 6, unroll=2)
        rest = 1.0 - guess
        score_sums = [jnp.sum(v, axis=0, keepdims=True) for v in (gx, gy, g * th2, g)]
        fisher_sums = [rest * jnp.sum(v, axis=0, keepdims=True) for v in (hx, hy, h * (th2 * th2), h)]
        out_ref[block] += jnp.concatenate(score_sums + fisher_sums, axis=0)
        return carry

    lax.fori_loop(0, count_ref[b], slot, 0)


def gather_params(packed, takers, blocks_own):
    everyone = lax.all_gather(packed, "takers", axis=0, tiled=False)
    table = everyone.reshape(takers, 5, blocks_own, packed.shape[-1])
    return jnp.transpose(table, (1, 0, 2, 3)).reshape(5, takers * blocks_own, -1).astype(jnp.float32)


def combine_nodes(red):
    row_max = red[:, 0]
    top = lax.pmax(row_max, "nodes")
    sums = lax.psum(red[:, 1:5] * jnp.exp(row_max - top)[:, None], "nodes")
    log_norm = top + jnp.log(sums[:, 0])
    means = sums[:, 1:4] / sums[:, 0:1]
    return log_norm, means


def reduce_stats(dense):
    own = lax.psum_scatter(dense, "takers", scatter_dimension=0, tiled=True)
    return lax.psum(own, "nodes")


def local(slopes, intercepts, guessing, responses, tile_items, tile_count):
    rowblk, slots, tile, _ = responses.shape
    takers, parts = lax.axis_size("takers"), lax.axis_size("nodes")
    planes = SIDE // parts
    nodes_here = planes * SIDE * SIDE
    rows_y = planes * SIDE
    items_own = intercepts.shape[0]
    blocks_own = items_own // tile
    blocks = blocks_own * takers
    packed = jnp.concatenate([slopes, intercepts[None], guessing[None]], axis=0).reshape(5 * blocks_own, tile)
    table = gather_params(packed, takers, blocks_own)
    x0 = (lax.axis_index("nodes") * planes).astype(jnp.int32).reshape(1)

    resp_spec = pl.BlockSpec((1, slots, tile, tile), lambda b, *_: (b, 0, 0, 0))
    table_spec = pl.BlockSpec((5, blocks, tile), lambda b, *_: (0, 0, 0))
    ll_spec = pl.BlockSpec((1, nodes_here, tile), lambda b, *_: (b, 0, 0))
    row_spec = pl.BlockSpec((1, 8, tile), lambda b, *_: (b, 0, 0))
    factors = [pltpu.VMEM((SIDE, tile), jnp.float32), pltpu.VMEM((rows_y, tile), jnp.float32)]
    params = pltpu.CompilerParams(vmem_limit_bytes=VMEM_LIMIT, dimension_semantics=("arbitrary",))
    elements = rowblk * slots * tile * nodes_here

    loglik, red = pl.pallas_call(
        functools.partial(loglik_kernel, planes),
        grid_spec=pltpu.PrefetchScalarGridSpec(
            num_scalar_prefetch=3, grid=(rowblk,), in_specs=[resp_spec, table_spec],
            out_specs=[ll_spec, row_spec], scratch_shapes=factors),
        out_shape=[jax.ShapeDtypeStruct((rowblk, nodes_here, tile), jnp.float32),
                   jax.ShapeDtypeStruct((rowblk, 8, tile), jnp.float32)],
        compiler_params=params,
        cost_estimate=pl.CostEstimate(flops=elements * 512, bytes_accessed=10 << 20, transcendentals=2 * elements),
    )(tile_items, tile_count, x0, responses, table)

    log_norm, means = combine_nodes(red)
    norm_rows = jnp.broadcast_to(log_norm[:, None, :], (rowblk, 8, tile))

    dense = pl.pallas_call(
        functools.partial(stats_kernel, planes),
        grid_spec=pltpu.PrefetchScalarGridSpec(
            num_scalar_prefetch=3, grid=(rowblk,), in_specs=[resp_spec, table_spec, ll_spec, row_spec],
            out_specs=pl.BlockSpec((blocks, 8, tile), lambda b, *_: (0, 0, 0)),
            scratch_shapes=factors + [pltpu.VMEM((nodes_here, tile), jnp.bfloat16)]),
        out_shape=jax.ShapeDtypeStruct((blocks, 8, tile), jnp.float32),
        compiler_params=params,
        cost_estimate=pl.CostEstimate(flops=elements * 512, bytes_accessed=12 << 20, transcendentals=elements),
    )(tile_items, tile_count, x0, responses, table, loglik, norm_rows)

    own = reduce_stats(dense)
    summed = jnp.transpose(own, (1, 0, 2)).reshape(8, items_own)
    current = jnp.concatenate([slopes.astype(jnp.float32), intercepts.astype(jnp.float32)[None]], axis=0)
    new_params = current + summed[:4] / (summed[4:] + 1.0)
    marginal = log_norm.reshape(rowblk * tile)
    posterior_mean = jnp.transpose(means, (1, 0, 2)).reshape(3, rowblk * tile)
    return new_params, marginal, posterior_mean


def solution(mesh):
    in_specs = (
        P(None, "takers"),
        P("takers"),
        P("takers"),
        P("takers", None, None, None),
        P("takers", None),
        P("takers"),
    )
    out_specs = (P(None, "takers"), P("takers"), P(None, "takers"))
    return jax.shard_map(local, mesh=mesh, in_specs=in_specs, out_specs=out_specs, check_vma=False)
```

```python
import functools

import jax
import jax.numpy as jnp
from jax import lax
from jax.experimental import pallas as pl
from jax.experimental.pallas import tpu as pltpu
from jax.sharding import PartitionSpec as P

SIDE = 16
STEP = 6.0 / (SIDE - 1)
MESH = pl.DeviceIdType.MESH
VMEM_LIMIT = 56 * 1024 * 1024


def lattice_point(index):
    return -3.0 + 6.0 * index.astype(jnp.float32) / (SIDE - 1)


def item_rows(tab_ref, block):
    return [tab_ref[p, pl.ds(block, 1), :] for p in range(5)]


def exp_factors(rows, x0, planes, ey_ref, w_ref):
    a0, a1, a2, d, _ = rows
    line = lattice_point(lax.broadcasted_iota(jnp.int32, (SIDE, a0.shape[1]), 0))
    ey_ref[...] = jnp.exp(a1 * line)
    ez = jnp.exp(a2 * line + d)
    ex = jnp.exp(a0 * lattice_point(x0 + lax.broadcasted_iota(jnp.int32, (SIDE, a0.shape[1]), 0)))
    for x in range(planes):
        w_ref[x * SIDE:(x + 1) * SIDE, :] = ez * ex[x:x + 1, :]


def row_index(shape):
    return lax.broadcasted_iota(jnp.int32, shape, 0)


def loglik_kernel(planes, items_ref, count_ref, x0_ref, resp_ref, tab_ref, ll_ref, red_ref, ey_ref, w_ref):
    b = pl.program_id(0)
    x0 = x0_ref[0]
    rows_y = planes * SIDE
    lanes = resp_ref.shape[-1]
    line = lattice_point(row_index((SIDE, lanes)))
    log_total = 3.0 * jnp.log(jnp.sum(jnp.exp(-0.5 * line * line), axis=0, keepdims=True))
    within = row_index((rows_y, lanes))
    th0 = lattice_point(x0 + within // SIDE)
    th2 = lattice_point(within % SIDE)
    prior_xz = -0.5 * (th0 * th0 + th2 * th2) - log_total

    def init(y, carry):
        th1 = lattice_point(jnp.full((1, lanes), y, jnp.int32))
        ll_ref[0, pl.ds(pl.multiple_of(y * rows_y, rows_y), rows_y), :] = prior_xz - 0.5 * th1 * th1
        return carry

    lax.fori_loop(0, SIDE, init, 0)

    def slot(k, carry):
        rows = item_rows(tab_ref, items_ref[b, k])
        exp_factors(rows, x0, planes, ey_ref, w_ref)
        guess = rows[4]
        log_rest = jnp.log(1.0 - guess)
        codes = resp_ref[0, k]
        ind = jnp.concatenate([(codes == 2).astype(jnp.bfloat16), (codes == 1).astype(jnp.bfloat16)], axis=1)

        def chunk(y, carry):
            u = w_ref[...] * ey_ref[pl.ds(y, 1), :]
            log_all = jnp.log(1.0 + u)
            log_right = jnp.log(guess + u) - log_all
            log_wrong = log_rest - log_all
            table = jnp.concatenate([log_right.astype(jnp.bfloat16), log_wrong.astype(jnp.bfloat16)], axis=1)
            part = lax.dot_general(table, ind, (((1,), (1,)), ((), ())), preferred_element_type=jnp.float32)
            ll_ref[0, pl.ds(pl.multiple_of(y * rows_y, rows_y), rows_y), :] += part
            return carry

        return lax.fori_loop(0, SIDE, chunk, carry, unroll=4)

    lax.fori_loop(0, count_ref[b], slot, 0)

    row_max = jnp.max(ll_ref[0], axis=0, keepdims=True)
    zero = jnp.zeros((rows_y, lanes), jnp.float32)

    def weigh(y, carry):
        total, by_y = carry
        w = jnp.exp(ll_ref[0, pl.ds(pl.multiple_of(y * rows_y, rows_y), rows_y), :] - row_max)
        th1 = lattice_point(jnp.full((1, lanes), y, jnp.int32))
        return total + w, by_y + w * th1

    total, by_y = lax.fori_loop(0, SIDE, weigh, (zero, zero))
    sums = [total, total * th0, by_y, total * th2]
    red_ref[0] = jnp.concatenate(
        [row_max] + [jnp.sum(s, axis=0, keepdims=True) for s in sums] + [jnp.zeros((3, lanes), jnp.float32)], axis=0)


def stats_kernel(planes, items_ref, count_ref, x0_ref, resp_ref, tab_ref, ll_ref, norm_ref, out_ref, ey_ref, w_ref, post_ref):
    b = pl.program_id(0)
    x0 = x0_ref[0]
    rows_y = planes * SIDE
    lanes = resp_ref.shape[-1]

    @pl.when(b == 0)
    def _():
        out_ref[...] = jnp.zeros_like(out_ref)

    log_norm = norm_ref[0, 0:1, :]
    post_ref[...] = jnp.exp(ll_ref[0] - log_norm).astype(jnp.bfloat16)
    th2 = lattice_point(row_index((SIDE, lanes)))

    def slot(k, carry):
        block = items_ref[b, k]
        rows = item_rows(tab_ref, block)
        exp_factors(rows, x0, planes, ey_ref, w_ref)
        guess = rows[4]
        codes = resp_ref[0, k]
        ind = jnp.concatenate([(codes == 2).astype(jnp.bfloat16), (codes > 0).astype(jnp.bfloat16)], axis=1)
        zero = jnp.zeros((SIDE, lanes), jnp.float32)

        def chunk(y, sums):
            post = post_ref[pl.ds(pl.multiple_of(y * rows_y, rows_y), rows_y), :]
            both = jnp.dot(post, ind, preferred_element_type=jnp.float32)
            e1 = ey_ref[pl.ds(y, 1), :]
            th1 = lattice_point(jnp.full((1, lanes), y, jnp.int32))
            s0 = s1 = f0 = f1 = zero
            for x in range(planes):
                lo, hi = x * SIDE, (x + 1) * SIDE
                hits, mass = both[lo:hi, :lanes], both[lo:hi, lanes:]
                u = w_ref[lo:hi, :] * e1
                cu, u1 = guess + u, 1.0 + u
                uk = u * pl.reciprocal(cu * u1)
                mc = mass * cu
                score = (hits * u1 - mc) * uk
                fisher = mc * (uk * uk)
                th0 = -3.0 + STEP * (x0 + x).astype(jnp.float32)
                s0, f0 = s0 + score, f0 + fisher
                s1, f1 = s1 + score * th0, f1 + fisher * (th0 * th0)
            g, gy, gx, h, hy, hx = sums
            return g + s0, gy + s0 * th1, gx + s1, h + f0, hy + f0 * (th1 * th1), hx + f1

        g, gy, gx, h, hy, hx = lax.fori_loop(0, SIDE, chunk, (zero,) * 6, unroll=2)
        rest = 1.0 - guess
        score_sums = [jnp.sum(v, axis=0, keepdims=True) for v in (gx, gy, g * th2, g)]
        fisher_sums = [rest * jnp.sum(v, axis=0, keepdims=True) for v in (hx, hy, h * (th2 * th2), h)]
        out_ref[block] += jnp.concatenate(score_sums + fisher_sums, axis=0)
        return carry

    lax.fori_loop(0, count_ref[b], slot, 0)


def enter(me, takers, core):
    barrier = pltpu.get_barrier_semaphore()

    def greet(o, carry):
        pl.semaphore_signal(barrier, inc=1, device_id=(lax.rem(me + o, takers), core), device_id_type=MESH)
        return carry

    lax.fori_loop(1, takers, greet, 0)
    pl.semaphore_signal(barrier, inc=1, device_id=(me, 1 - core), device_id_type=MESH)
    pl.semaphore_wait(barrier, takers)


def gather_kernel(takers, mine_ref, tab_ref, held, send1, recv1, send2, recv2):
    me, core = lax.axis_index("takers"), lax.axis_index("nodes")
    rows = mine_ref.shape[0]
    half = rows // 2
    own = rows // 5
    here = pl.ds(pl.multiple_of(core * half, half), half)
    enter(me, takers, core)

    def away(o):
        return pltpu.make_async_remote_copy(
            src_ref=mine_ref.at[here, :], dst_ref=held.at[me, here, :], send_sem=send1.at[o], recv_sem=recv1.at[o],
            device_id=(lax.rem(me + o, takers), core), device_id_type=MESH)

    def across(o):
        part = held.at[lax.rem(me + takers - o, takers), here, :]
        return pltpu.make_async_remote_copy(
            src_ref=part, dst_ref=part, send_sem=send2.at[o], recv_sem=recv2.at[o],
            device_id=(me, 1 - core), device_id_type=MESH)

    def spread(source, value):
        for p in range(5):
            tab_ref[p, pl.ds(pl.multiple_of(source * own, own), own), :] = value[p * own:(p + 1) * own].astype(jnp.float32)

    def begin(o, carry):
        away(o).start()
        return carry

    def forward(o, carry):
        away(o).wait_recv()
        across(o).start()
        return carry

    def finish(o, carry):
        across(o).wait_recv()
        source = lax.rem(me + takers - o, takers)
        spread(source, held[source])
        return carry

    def drain(o, carry):
        away(o).wait_send()
        across(o).wait_send()
        return carry

    lax.fori_loop(1, takers, begin, 0)
    spread(me, mine_ref[...])
    lax.fori_loop(1, takers, forward, 0)
    lax.fori_loop(1, takers, finish, 0)
    lax.fori_loop(1, takers, drain, 0)


def combine_kernel(red_ref, out_ref, theirs, send, recv):
    me, core = lax.axis_index("takers"), lax.axis_index("nodes")
    barrier = pltpu.get_barrier_semaphore()
    pl.semaphore_signal(barrier, inc=1, device_id=(me, 1 - core), device_id_type=MESH)
    pl.semaphore_wait(barrier, 1)
    copy = pltpu.make_async_remote_copy(
        src_ref=red_ref, dst_ref=theirs, send_sem=send, recv_sem=recv, device_id=(me, 1 - core), device_id_type=MESH)
    copy.start()
    copy.wait()
    for b in range(red_ref.shape[0]):
        a, t = red_ref[b], theirs[b]
        top = jnp.maximum(a[0:1], t[0:1])
        sums = a[1:5] * jnp.exp(a[0:1] - top) + t[1:5] * jnp.exp(t[0:1] - top)
        log_norm = top + jnp.log(sums[0:1])
        out_ref[b] = jnp.concatenate([log_norm, sums[1:4] / sums[0:1], jnp.zeros_like(a[4:])], axis=0)


def reduce_kernel(takers, dense_ref, out_ref, out1, in1, out2, in2, sum_out, sum_in,
                  send1, recv1, send2, recv2, send3, recv3):
    me, core = lax.axis_index("takers"), lax.axis_index("nodes")
    half = out1.shape[1]

    def piece(owner, side):
        return pl.ds(pl.multiple_of((owner * 2 + side) * half, half), half)

    def across(o):
        owner = lax.rem(me + o, takers)
        return pltpu.make_async_remote_copy(
            src_ref=out1.at[owner], dst_ref=in1.at[owner], send_sem=send1.at[o], recv_sem=recv1.at[o],
            device_id=(me, 1 - core), device_id_type=MESH)

    def away(o):
        owner = lax.rem(me + o, takers)
        return pltpu.make_async_remote_copy(
            src_ref=out2.at[owner], dst_ref=in2.at[me], send_sem=send2.at[o], recv_sem=recv2.at[o],
            device_id=(owner, core), device_id_type=MESH)

    def both(owner):
        return dense_ref[piece(owner, core), :] + in1[owner].astype(jnp.float32)

    def begin(o, carry):
        owner = lax.rem(me + o, takers)
        out1[owner] = dense_ref[piece(owner, 1 - core), :].astype(jnp.bfloat16)
        across(o).start()
        return carry

    def forward(o, carry):
        owner = lax.rem(me + o, takers)
        across(o).wait_recv()
        out2[owner] = both(owner).astype(jnp.bfloat16)
        away(o).start()
        return carry

    def add(o, carry):
        away(o).wait_recv()
        sum_out[...] += in2[lax.rem(me + takers - o, takers)].astype(jnp.float32)
        return carry

    def drain(o, carry):
        across(o).wait_send()
        away(o).wait_send()
        return carry

    enter(me, takers, core)
    lax.fori_loop(1, takers, begin, 0)
    begin(0, 0)
    lax.fori_loop(1, takers, forward, 0)
    across(0).wait_recv()
    sum_out[...] = both(me)
    lax.fori_loop(1, takers, add, 0)
    last = pltpu.make_async_remote_copy(
        src_ref=sum_out, dst_ref=sum_in, send_sem=send3, recv_sem=recv3, device_id=(me, 1 - core), device_id_type=MESH)
    last.start()
    out_ref[pl.ds(pl.multiple_of(core * half, half), half), :] = sum_out[...]
    lax.fori_loop(1, takers, drain, 0)
    across(0).wait_send()
    last.wait()
    out_ref[pl.ds(pl.multiple_of((1 - core) * half, half), half), :] = sum_in[...]


def remote_call(kernel, collective_id, out_shape, scratch, nbytes, *args):
    vmem = pl.BlockSpec(memory_space=pltpu.VMEM)
    return pl.pallas_call(
        kernel, out_shape=out_shape, in_specs=[vmem] * len(args), out_specs=vmem, scratch_shapes=scratch,
        compiler_params=pltpu.CompilerParams(
            collective_id=collective_id, has_side_effects=True, vmem_limit_bytes=VMEM_LIMIT),
        cost_estimate=pl.CostEstimate(flops=0, bytes_accessed=nbytes, transcendentals=0))(*args)


def paired(rows):
    return lax.axis_size("nodes") == 2 and rows % 32 == 0


def gather_params(packed, takers, blocks_own):
    rows, lanes = packed.shape
    if paired(rows):
        sems = [pltpu.SemaphoreType.DMA((takers,))] * 4
        return remote_call(
            functools.partial(gather_kernel, takers), 0,
            jax.ShapeDtypeStruct((5, takers * blocks_own, lanes), jnp.float32),
            [pltpu.VMEM((takers, rows, lanes), jnp.bfloat16)] + sems, 4 << 20, packed)
    everyone = lax.all_gather(packed, "takers", axis=0, tiled=False)
    table = everyone.reshape(takers, 5, blocks_own, lanes)
    return jnp.transpose(table, (1, 0, 2, 3)).reshape(5, takers * blocks_own, lanes).astype(jnp.float32)


def combine_nodes(red):
    if lax.axis_size("nodes") == 2:
        return remote_call(
            combine_kernel, 1, jax.ShapeDtypeStruct(red.shape, jnp.float32),
            [pltpu.VMEM(red.shape, jnp.float32), pltpu.SemaphoreType.DMA, pltpu.SemaphoreType.DMA], 1 << 16, red)
    row_max = red[:, 0:1]
    top = lax.pmax(row_max, "nodes")
    sums = lax.psum(red[:, 1:5] * jnp.exp(row_max - top), "nodes")
    log_norm = top + jnp.log(sums[:, 0:1])
    return jnp.concatenate([log_norm, sums[:, 1:4] / sums[:, 0:1], jnp.zeros_like(red[:, 4:])], axis=1)


def reduce_stats(dense, takers):
    blocks, rows, lanes = dense.shape
    own = blocks // takers
    if paired(own * rows):
        half = own * rows // 2
        pieces = pltpu.VMEM((takers, half, lanes), jnp.bfloat16)
        total = pltpu.VMEM((half, lanes), jnp.float32)
        scratch = [pieces] * 4 + [total] * 2 + [pltpu.SemaphoreType.DMA((takers,))] * 4 + [pltpu.SemaphoreType.DMA] * 2
        summed = remote_call(
            functools.partial(reduce_kernel, takers), 2, jax.ShapeDtypeStruct((own * rows, lanes), jnp.float32),
            scratch, 8 << 20, dense.reshape(blocks * rows, lanes))
        return summed.reshape(own, rows, lanes)
    return lax.psum(lax.psum_scatter(dense, "takers", scatter_dimension=0, tiled=True), "nodes")


def local(slopes, intercepts, guessing, responses, tile_items, tile_count):
    rowblk, slots, tile, _ = responses.shape
    takers, parts = lax.axis_size("takers"), lax.axis_size("nodes")
    planes = SIDE // parts
    nodes_here = planes * SIDE * SIDE
    rows_y = planes * SIDE
    items_own = intercepts.shape[0]
    blocks_own = items_own // tile
    blocks = blocks_own * takers
    packed = jnp.concatenate([slopes, intercepts[None], guessing[None]], axis=0).reshape(5 * blocks_own, tile)
    table = gather_params(packed, takers, blocks_own)
    x0 = (lax.axis_index("nodes") * planes).astype(jnp.int32).reshape(1)

    resp_spec = pl.BlockSpec((1, slots, tile, tile), lambda b, *_: (b, 0, 0, 0))
    table_spec = pl.BlockSpec((5, blocks, tile), lambda b, *_: (0, 0, 0))
    ll_spec = pl.BlockSpec((1, nodes_here, tile), lambda b, *_: (b, 0, 0))
    row_spec = pl.BlockSpec((1, 8, tile), lambda b, *_: (b, 0, 0))
    factors = [pltpu.VMEM((SIDE, tile), jnp.float32), pltpu.VMEM((rows_y, tile), jnp.float32)]
    params = pltpu.CompilerParams(vmem_limit_bytes=VMEM_LIMIT, dimension_semantics=("arbitrary",))
    elements = rowblk * slots * tile * nodes_here

    loglik, red = pl.pallas_call(
        functools.partial(loglik_kernel, planes),
        grid_spec=pltpu.PrefetchScalarGridSpec(
            num_scalar_prefetch=3, grid=(rowblk,), in_specs=[resp_spec, table_spec],
            out_specs=[ll_spec, row_spec], scratch_shapes=factors),
        out_shape=[jax.ShapeDtypeStruct((rowblk, nodes_here, tile), jnp.float32),
                   jax.ShapeDtypeStruct((rowblk, 8, tile), jnp.float32)],
        compiler_params=params,
        cost_estimate=pl.CostEstimate(flops=elements * 512, bytes_accessed=10 << 20, transcendentals=2 * elements),
    )(tile_items, tile_count, x0, responses, table)

    norm_rows = combine_nodes(red)

    dense = pl.pallas_call(
        functools.partial(stats_kernel, planes),
        grid_spec=pltpu.PrefetchScalarGridSpec(
            num_scalar_prefetch=3, grid=(rowblk,), in_specs=[resp_spec, table_spec, ll_spec, row_spec],
            out_specs=pl.BlockSpec((blocks, 8, tile), lambda b, *_: (0, 0, 0)),
            scratch_shapes=factors + [pltpu.VMEM((nodes_here, tile), jnp.bfloat16)]),
        out_shape=jax.ShapeDtypeStruct((blocks, 8, tile), jnp.float32),
        compiler_params=params,
        cost_estimate=pl.CostEstimate(flops=elements * 512, bytes_accessed=12 << 20, transcendentals=elements),
    )(tile_items, tile_count, x0, responses, table, loglik, norm_rows)

    own = reduce_stats(dense, takers)
    summed = jnp.transpose(own, (1, 0, 2)).reshape(8, items_own)
    current = jnp.concatenate([slopes.astype(jnp.float32), intercepts.astype(jnp.float32)[None]], axis=0)
    new_params = current + summed[:4] / (summed[4:] + 1.0)
    marginal = norm_rows[:, 0].reshape(rowblk * tile)
    posterior_mean = jnp.transpose(norm_rows[:, 1:4], (1, 0, 2)).reshape(3, rowblk * tile)
    return new_params, marginal, posterior_mean


def solution(mesh):
    in_specs = (
        P(None, "takers"),
        P("takers"),
        P("takers"),
        P("takers", None, None, None),
        P("takers", None),
        P("takers"),
    )
    out_specs = (P(None, "takers"), P("takers"), P(None, "takers"))
    return jax.shard_map(local, mesh=mesh, in_specs=in_specs, out_specs=out_specs, check_vma=False)
```

```python
import functools

import jax
import jax.numpy as jnp
from jax import lax
from jax.experimental import pallas as pl
from jax.experimental.pallas import tpu as pltpu
from jax.sharding import PartitionSpec as P

SIDE = 16
STEP = 6.0 / (SIDE - 1)
MESH = pl.DeviceIdType.MESH
VMEM_LIMIT = 56 * 1024 * 1024


def lattice_point(index):
    return -3.0 + 6.0 * index.astype(jnp.float32) / (SIDE - 1)


def item_rows(tab_ref, block):
    return [tab_ref[p, pl.ds(block, 1), :] for p in range(5)]


def exp_factors(rows, x0, planes, ey_ref, w_ref):
    a0, a1, a2, d, _ = rows
    line = lattice_point(lax.broadcasted_iota(jnp.int32, (SIDE, a0.shape[1]), 0))
    ey_ref[...] = jnp.exp(a1 * line)
    ez = jnp.exp(a2 * line + d)
    ex = jnp.exp(a0 * lattice_point(x0 + lax.broadcasted_iota(jnp.int32, (SIDE, a0.shape[1]), 0)))
    for x in range(planes):
        w_ref[x * SIDE:(x + 1) * SIDE, :] = ez * ex[x:x + 1, :]


def row_index(shape):
    return lax.broadcasted_iota(jnp.int32, shape, 0)


def loglik_kernel(planes, items_ref, count_ref, x0_ref, resp_ref, tab_ref, ll_ref, red_ref, ey_ref, w_ref):
    b = pl.program_id(0)
    x0 = x0_ref[0]
    rows_y = planes * SIDE
    lanes = resp_ref.shape[-1]
    line = lattice_point(row_index((SIDE, lanes)))
    log_total = 3.0 * jnp.log(jnp.sum(jnp.exp(-0.5 * line * line), axis=0, keepdims=True))
    within = row_index((rows_y, lanes))
    th0 = lattice_point(x0 + within // SIDE)
    th2 = lattice_point(within % SIDE)
    prior_xz = -0.5 * (th0 * th0 + th2 * th2) - log_total

    def init(y, carry):
        th1 = lattice_point(jnp.full((1, lanes), y, jnp.int32))
        ll_ref[0, pl.ds(pl.multiple_of(y * rows_y, rows_y), rows_y), :] = prior_xz - 0.5 * th1 * th1
        return carry

    lax.fori_loop(0, SIDE, init, 0)

    def slot(k, carry):
        rows = item_rows(tab_ref, items_ref[b, k])
        exp_factors(rows, x0, planes, ey_ref, w_ref)
        guess = rows[4]
        log_rest = jnp.log(1.0 - guess)
        codes = resp_ref[0, k].T
        ind = jnp.concatenate([(codes == 2).astype(jnp.bfloat16), (codes == 1).astype(jnp.bfloat16)], axis=0)

        def chunk(y, carry):
            u = w_ref[...] * ey_ref[pl.ds(y, 1), :]
            log_all = jnp.log(1.0 + u)
            log_right = jnp.log(guess + u) - log_all
            log_wrong = log_rest - log_all
            table = jnp.concatenate([log_right.astype(jnp.bfloat16), log_wrong.astype(jnp.bfloat16)], axis=1)
            part = jnp.dot(table, ind, preferred_element_type=jnp.float32)
            ll_ref[0, pl.ds(pl.multiple_of(y * rows_y, rows_y), rows_y), :] += part
            return carry

        return lax.fori_loop(0, SIDE, chunk, carry, unroll=16)

    lax.fori_loop(0, count_ref[b], slot, 0)

    row_max = jnp.max(ll_ref[0], axis=0, keepdims=True)
    zero = jnp.zeros((rows_y, lanes), jnp.float32)

    def weigh(y, carry):
        total, by_y = carry
        w = jnp.exp(ll_ref[0, pl.ds(pl.multiple_of(y * rows_y, rows_y), rows_y), :] - row_max)
        th1 = lattice_point(jnp.full((1, lanes), y, jnp.int32))
        return total + w, by_y + w * th1

    total, by_y = lax.fori_loop(0, SIDE, weigh, (zero, zero))
    sums = [total, total * th0, by_y, total * th2]
    red_ref[0] = jnp.concatenate(
        [row_max] + [jnp.sum(s, axis=0, keepdims=True) for s in sums] + [jnp.zeros((3, lanes), jnp.float32)], axis=0)


def stats_kernel(planes, items_ref, count_ref, x0_ref, resp_ref, tab_ref, ll_ref, norm_ref, out_ref, marg_ref, mean_ref, ey_ref, w_ref, post_ref):
    b = pl.program_id(0)
    x0 = x0_ref[0]
    rows_y = planes * SIDE
    lanes = resp_ref.shape[-1]

    @pl.when(b == 0)
    def _():
        out_ref[...] = jnp.zeros_like(out_ref)

    log_norm = norm_ref[0, 0:1, :]
    marg_ref[...] = log_norm
    mean_ref[...] = norm_ref[0, 1:4, :]
    post_ref[...] = jnp.exp(ll_ref[0] - log_norm).astype(jnp.bfloat16)
    th2 = lattice_point(row_index((SIDE, lanes)))

    def slot(k, carry):
        block = items_ref[b, k]
        rows = item_rows(tab_ref, block)
        exp_factors(rows, x0, planes, ey_ref, w_ref)
        guess = rows[4]
        codes = resp_ref[0, k]
        ind = jnp.concatenate([(codes == 2).astype(jnp.bfloat16), (codes > 0).astype(jnp.bfloat16)], axis=1)
        zero = jnp.zeros((SIDE, lanes), jnp.float32)

        def chunk(y, sums):
            post = post_ref[pl.ds(pl.multiple_of(y * rows_y, rows_y), rows_y), :]
            both = jnp.dot(post, ind, preferred_element_type=jnp.float32)
            e1 = ey_ref[pl.ds(y, 1), :]
            th1 = lattice_point(jnp.full((1, lanes), y, jnp.int32))
            s0 = s1 = f0 = f1 = f2 = zero
            for x in reversed(range(planes)):
                lo, hi = x * SIDE, (x + 1) * SIDE
                hits, mass = both[lo:hi, :lanes], both[lo:hi, lanes:]
                u = w_ref[lo:hi, :] * e1
                cu, u1 = guess + u, 1.0 + u
                under = cu * u1
                first = pl.reciprocal(under, approx=True)
                uk = (u * first) * (2.0 - under * first)
                mc = mass * cu
                s0 = s0 + (hits * u1 - mc) * uk
                f0 = f0 + mc * (uk * uk)
                if x > 0:
                    s1, f1 = s1 + s0, f1 + f0
                    f2 = f2 + f1
            low = -3.0 + STEP * x0.astype(jnp.float32)
            sx = low * s0 + STEP * s1
            fx = (low * low) * f0 + (2.0 * STEP * low - STEP * STEP) * f1 + (2.0 * STEP * STEP) * f2
            g, gy, gx, h, hy, hx = sums
            return g + s0, gy + s0 * th1, gx + sx, h + f0, hy + f0 * (th1 * th1), hx + fx

        g, gy, gx, h, hy, hx = lax.fori_loop(0, SIDE, chunk, (zero,) * 6, unroll=16)
        rest = 1.0 - guess
        score_sums = [jnp.sum(v, axis=0, keepdims=True) for v in (gx, gy, g * th2, g)]
        fisher_sums = [rest * jnp.sum(v, axis=0, keepdims=True) for v in (hx, hy, h * (th2 * th2), h)]
        out_ref[block] += jnp.concatenate(score_sums + fisher_sums, axis=0)
        return carry

    lax.fori_loop(0, count_ref[b], slot, 0)


def enter(me, takers, core):
    barrier = pltpu.get_barrier_semaphore()

    def greet(o, carry):
        pl.semaphore_signal(barrier, inc=1, device_id=(lax.rem(me + o, takers), core), device_id_type=MESH)
        return carry

    lax.fori_loop(1, takers, greet, 0)
    pl.semaphore_signal(barrier, inc=1, device_id=(me, 1 - core), device_id_type=MESH)
    pl.semaphore_wait(barrier, takers)


def gather_kernel(takers, slope_ref, icpt_ref, guess_ref, tab_ref, mine_ref, held, send1, recv1, send2, recv2):
    me, core = lax.axis_index("takers"), lax.axis_index("nodes")
    rows = mine_ref.shape[0]
    half = rows // 2
    own = rows // 5
    here = pl.ds(pl.multiple_of(core * half, half), half)
    mine_ref[0:3 * own, :] = slope_ref[...]
    mine_ref[3 * own:4 * own, :] = icpt_ref[...]
    mine_ref[4 * own:, :] = guess_ref[...]
    enter(me, takers, core)

    def away(o):
        return pltpu.make_async_remote_copy(
            src_ref=mine_ref.at[here, :], dst_ref=held.at[me, here, :], send_sem=send1.at[o], recv_sem=recv1.at[o],
            device_id=(lax.rem(me + o, takers), core), device_id_type=MESH)

    def across(o):
        part = held.at[lax.rem(me + takers - o, takers), here, :]
        return pltpu.make_async_remote_copy(
            src_ref=part, dst_ref=part, send_sem=send2.at[o], recv_sem=recv2.at[o],
            device_id=(me, 1 - core), device_id_type=MESH)

    def spread(source, value):
        for p in range(5):
            tab_ref[p, pl.ds(pl.multiple_of(source * own, own), own), :] = value[p * own:(p + 1) * own].astype(jnp.float32)

    def begin(o, carry):
        away(o).start()
        return carry

    def forward(o, carry):
        away(o).wait_recv()
        across(o).start()
        return carry

    def finish(o, carry):
        across(o).wait_recv()
        source = lax.rem(me + takers - o, takers)
        spread(source, held[source])
        return carry

    def drain(o, carry):
        away(o).wait_send()
        across(o).wait_send()
        return carry

    lax.fori_loop(1, takers, begin, 0)
    spread(me, mine_ref[...])
    lax.fori_loop(1, takers, forward, 0)
    lax.fori_loop(1, takers, finish, 0)
    lax.fori_loop(1, takers, drain, 0)


def combine_kernel(red_ref, out_ref, theirs, send, recv):
    me, core = lax.axis_index("takers"), lax.axis_index("nodes")
    barrier = pltpu.get_barrier_semaphore()
    pl.semaphore_signal(barrier, inc=1, device_id=(me, 1 - core), device_id_type=MESH)
    pl.semaphore_wait(barrier, 1)
    copy = pltpu.make_async_remote_copy(
        src_ref=red_ref, dst_ref=theirs, send_sem=send, recv_sem=recv, device_id=(me, 1 - core), device_id_type=MESH)
    copy.start()
    copy.wait()
    for b in range(red_ref.shape[0]):
        a, t = red_ref[b], theirs[b]
        top = jnp.maximum(a[0:1], t[0:1])
        sums = a[1:5] * jnp.exp(a[0:1] - top) + t[1:5] * jnp.exp(t[0:1] - top)
        log_norm = top + jnp.log(sums[0:1])
        out_ref[b] = jnp.concatenate([log_norm, sums[1:4] / sums[0:1], jnp.zeros_like(a[4:])], axis=0)


def reduce_kernel(takers, dense_ref, out_ref, out1, in1, out2, in2, sum_out, sum_in,
                  send1, recv1, send2, recv2, send3, recv3):
    me, core = lax.axis_index("takers"), lax.axis_index("nodes")
    half = out1.shape[1]

    def piece(owner, side):
        return pl.ds(pl.multiple_of((owner * 2 + side) * half, half), half)

    def across(o):
        owner = lax.rem(me + o, takers)
        return pltpu.make_async_remote_copy(
            src_ref=out1.at[owner], dst_ref=in1.at[owner], send_sem=send1.at[o], recv_sem=recv1.at[o],
            device_id=(me, 1 - core), device_id_type=MESH)

    def away(o):
        owner = lax.rem(me + o, takers)
        return pltpu.make_async_remote_copy(
            src_ref=out2.at[owner], dst_ref=in2.at[me], send_sem=send2.at[o], recv_sem=recv2.at[o],
            device_id=(owner, core), device_id_type=MESH)

    def both(owner):
        return dense_ref[piece(owner, core), :] + in1[owner].astype(jnp.float32)

    def begin(o, carry):
        owner = lax.rem(me + o, takers)
        out1[owner] = dense_ref[piece(owner, 1 - core), :].astype(jnp.bfloat16)
        across(o).start()
        return carry

    def forward(o, carry):
        owner = lax.rem(me + o, takers)
        across(o).wait_recv()
        out2[owner] = both(owner).astype(jnp.bfloat16)
        away(o).start()
        return carry

    def add(o, carry):
        away(o).wait_recv()
        sum_out[...] += in2[lax.rem(me + takers - o, takers)].astype(jnp.float32)
        return carry

    def drain(o, carry):
        across(o).wait_send()
        away(o).wait_send()
        return carry

    enter(me, takers, core)
    lax.fori_loop(1, takers, begin, 0)
    begin(0, 0)
    lax.fori_loop(1, takers, forward, 0)
    across(0).wait_recv()
    sum_out[...] = both(me)
    lax.fori_loop(1, takers, add, 0)
    last = pltpu.make_async_remote_copy(
        src_ref=sum_out, dst_ref=sum_in, send_sem=send3, recv_sem=recv3, device_id=(me, 1 - core), device_id_type=MESH)
    last.start()
    out_ref[pl.ds(pl.multiple_of(core * half, half), half), :] = sum_out[...]
    lax.fori_loop(1, takers, drain, 0)
    across(0).wait_send()
    last.wait()
    out_ref[pl.ds(pl.multiple_of((1 - core) * half, half), half), :] = sum_in[...]


def remote_call(kernel, collective_id, out_shape, scratch, nbytes, *args):
    vmem = pl.BlockSpec(memory_space=pltpu.VMEM)
    return pl.pallas_call(
        kernel, out_shape=out_shape, in_specs=[vmem] * len(args), out_specs=vmem, scratch_shapes=scratch,
        compiler_params=pltpu.CompilerParams(
            collective_id=collective_id, has_side_effects=True, vmem_limit_bytes=VMEM_LIMIT),
        cost_estimate=pl.CostEstimate(flops=0, bytes_accessed=nbytes, transcendentals=0))(*args)


def paired(rows):
    return lax.axis_size("nodes") == 2 and rows % 32 == 0


def gather_params(slopes, intercepts, guessing, takers, lanes):
    blocks_own = intercepts.shape[0] // lanes
    rows = 5 * blocks_own
    if paired(rows) and blocks_own % 16 == 0:
        sems = [pltpu.SemaphoreType.DMA((takers,))] * 4
        return remote_call(
            functools.partial(gather_kernel, takers), 0,
            jax.ShapeDtypeStruct((5, takers * blocks_own, lanes), jnp.float32),
            [pltpu.VMEM((rows, lanes), jnp.bfloat16), pltpu.VMEM((takers, rows, lanes), jnp.bfloat16)] + sems, 4 << 20,
            slopes.reshape(3 * blocks_own, lanes), intercepts.reshape(blocks_own, lanes),
            guessing.reshape(blocks_own, lanes))
    packed = jnp.concatenate([slopes, intercepts[None], guessing[None]], axis=0).reshape(rows, lanes)
    everyone = lax.all_gather(packed, "takers", axis=0, tiled=False)
    table = everyone.reshape(takers, 5, blocks_own, lanes)
    return jnp.transpose(table, (1, 0, 2, 3)).reshape(5, takers * blocks_own, lanes).astype(jnp.float32)


def combine_nodes(red):
    if lax.axis_size("nodes") == 2:
        return remote_call(
            combine_kernel, 1, jax.ShapeDtypeStruct(red.shape, jnp.float32),
            [pltpu.VMEM(red.shape, jnp.float32), pltpu.SemaphoreType.DMA, pltpu.SemaphoreType.DMA], 1 << 16, red)
    row_max = red[:, 0:1]
    top = lax.pmax(row_max, "nodes")
    sums = lax.psum(red[:, 1:5] * jnp.exp(row_max - top), "nodes")
    log_norm = top + jnp.log(sums[:, 0:1])
    return jnp.concatenate([log_norm, sums[:, 1:4] / sums[:, 0:1], jnp.zeros_like(red[:, 4:])], axis=1)


def reduce_stats(dense, takers):
    blocks, rows, lanes = dense.shape
    own = blocks // takers
    if paired(own * rows):
        half = own * rows // 2
        pieces = pltpu.VMEM((takers, half, lanes), jnp.bfloat16)
        total = pltpu.VMEM((half, lanes), jnp.float32)
        scratch = [pieces] * 4 + [total] * 2 + [pltpu.SemaphoreType.DMA((takers,))] * 4 + [pltpu.SemaphoreType.DMA] * 2
        summed = remote_call(
            functools.partial(reduce_kernel, takers), 2, jax.ShapeDtypeStruct((own * rows, lanes), jnp.float32),
            scratch, 8 << 20, dense.reshape(blocks * rows, lanes))
        return summed.reshape(own, rows, lanes)
    return lax.psum(lax.psum_scatter(dense, "takers", scatter_dimension=0, tiled=True), "nodes")


def local(slopes, intercepts, guessing, responses, tile_items, tile_count):
    rowblk, slots, tile, _ = responses.shape
    takers, parts = lax.axis_size("takers"), lax.axis_size("nodes")
    planes = SIDE // parts
    nodes_here = planes * SIDE * SIDE
    rows_y = planes * SIDE
    items_own = intercepts.shape[0]
    blocks_own = items_own // tile
    blocks = blocks_own * takers
    table = gather_params(slopes, intercepts, guessing, takers, tile)
    x0 = (lax.axis_index("nodes") * planes).astype(jnp.int32).reshape(1)

    resp_spec = pl.BlockSpec((1, slots, tile, tile), lambda b, *_: (b, 0, 0, 0))
    table_spec = pl.BlockSpec((5, blocks, tile), lambda b, *_: (0, 0, 0))
    ll_spec = pl.BlockSpec((1, nodes_here, tile), lambda b, *_: (b, 0, 0))
    row_spec = pl.BlockSpec((1, 8, tile), lambda b, *_: (b, 0, 0))
    factors = [pltpu.VMEM((SIDE, tile), jnp.float32), pltpu.VMEM((rows_y, tile), jnp.float32)]
    params = pltpu.CompilerParams(vmem_limit_bytes=VMEM_LIMIT, dimension_semantics=("arbitrary",))
    elements = rowblk * slots * tile * nodes_here

    loglik, red = pl.pallas_call(
        functools.partial(loglik_kernel, planes),
        grid_spec=pltpu.PrefetchScalarGridSpec(
            num_scalar_prefetch=3, grid=(rowblk,), in_specs=[resp_spec, table_spec],
            out_specs=[ll_spec, row_spec], scratch_shapes=factors),
        out_shape=[jax.ShapeDtypeStruct((rowblk, nodes_here, tile), jnp.float32),
                   jax.ShapeDtypeStruct((rowblk, 8, tile), jnp.float32)],
        compiler_params=params,
        cost_estimate=pl.CostEstimate(flops=elements * 512, bytes_accessed=10 << 20, transcendentals=2 * elements),
    )(tile_items, tile_count, x0, responses, table)

    norm_rows = combine_nodes(red)

    dense, marginal, posterior_mean = pl.pallas_call(
        functools.partial(stats_kernel, planes),
        grid_spec=pltpu.PrefetchScalarGridSpec(
            num_scalar_prefetch=3, grid=(rowblk,), in_specs=[resp_spec, table_spec, ll_spec, row_spec],
            out_specs=[pl.BlockSpec((blocks, 8, tile), lambda b, *_: (0, 0, 0)),
                       pl.BlockSpec((1, tile), lambda b, *_: (0, b)),
                       pl.BlockSpec((3, tile), lambda b, *_: (0, b))],
            scratch_shapes=factors + [pltpu.VMEM((nodes_here, tile), jnp.bfloat16)]),
        out_shape=[jax.ShapeDtypeStruct((blocks, 8, tile), jnp.float32),
                   jax.ShapeDtypeStruct((1, rowblk * tile), jnp.float32),
                   jax.ShapeDtypeStruct((3, rowblk * tile), jnp.float32)],
        compiler_params=params,
        cost_estimate=pl.CostEstimate(flops=elements * 512, bytes_accessed=12 << 20, transcendentals=elements),
    )(tile_items, tile_count, x0, responses, table, loglik, norm_rows)

    own = reduce_stats(dense, takers)
    summed = jnp.transpose(own, (1, 0, 2)).reshape(8, items_own)
    current = jnp.concatenate([slopes.astype(jnp.float32), intercepts.astype(jnp.float32)[None]], axis=0)
    new_params = current + summed[:4] / (summed[4:] + 1.0)
    return new_params, marginal.reshape(rowblk * tile), posterior_mean


def solution(mesh):
    in_specs = (
        P(None, "takers"),
        P("takers"),
        P("takers"),
        P("takers", None, None, None),
        P("takers", None),
        P("takers"),
    )
    out_specs = (P(None, "takers"), P("takers"), P(None, "takers"))
    return jax.shard_map(local, mesh=mesh, in_specs=in_specs, out_specs=out_specs, check_vma=False)
```

```python
import functools

import jax
import jax.numpy as jnp
from jax import lax
from jax.experimental import pallas as pl
from jax.experimental.pallas import tpu as pltpu
from jax.sharding import PartitionSpec as P

SIDE = 16
STEP = 6.0 / (SIDE - 1)
MESH = pl.DeviceIdType.MESH
VMEM_LIMIT = 56 * 1024 * 1024


def lattice_point(index):
    return -3.0 + 6.0 * index.astype(jnp.float32) / (SIDE - 1)


def item_rows(tab_ref, block):
    return [tab_ref[p, pl.ds(block, 1), :] for p in range(5)]


def each_pair(count, tiles):
    def pair(p, carry):
        tiles([2 * p, 2 * p + 1])
        return carry

    lax.fori_loop(0, count // 2, pair, 0)

    @pl.when(count % 2 == 1)
    def _():
        tiles([count - 1])


def exp_factors(rows, x0, planes, ey_ref, w_ref):
    a0, a1, a2, d, _ = rows
    line = lattice_point(lax.broadcasted_iota(jnp.int32, (SIDE, a0.shape[1]), 0))
    ey_ref[...] = jnp.exp(a1 * line)
    ez = jnp.exp(a2 * line + d)
    ex = jnp.exp(a0 * lattice_point(x0 + lax.broadcasted_iota(jnp.int32, (SIDE, a0.shape[1]), 0)))
    for x in range(planes):
        w_ref[x * SIDE:(x + 1) * SIDE, :] = ez * ex[x:x + 1, :]


def row_index(shape):
    return lax.broadcasted_iota(jnp.int32, shape, 0)


def loglik_kernel(planes, items_ref, count_ref, x0_ref, resp_ref, tab_ref, ll_ref, red_ref, ey_ref, w_ref):
    b = pl.program_id(0)
    x0 = x0_ref[0]
    rows_y = planes * SIDE
    lanes = resp_ref.shape[-1]
    line = lattice_point(row_index((SIDE, lanes)))
    log_total = 3.0 * jnp.log(jnp.sum(jnp.exp(-0.5 * line * line), axis=0, keepdims=True))
    within = row_index((rows_y, lanes))
    th0 = lattice_point(x0 + within // SIDE)
    th2 = lattice_point(within % SIDE)
    prior_xz = -0.5 * (th0 * th0 + th2 * th2) - log_total

    def init(y, carry):
        th1 = lattice_point(jnp.full((1, lanes), y, jnp.int32))
        ll_ref[0, pl.ds(pl.multiple_of(y * rows_y, rows_y), rows_y), :] = prior_xz - 0.5 * th1 * th1
        return carry

    lax.fori_loop(0, SIDE, init, 0, unroll=4)

    def tiles(ks):
        guess, log_rest, ind = [], [], []
        for j, k in enumerate(ks):
            rows = item_rows(tab_ref, items_ref[b, k])
            exp_factors(rows, x0, planes, ey_ref.at[j], w_ref.at[j])
            guess.append(rows[4])
            log_rest.append(jnp.log(1.0 - rows[4]))
            codes = resp_ref[0, k].T
            ind += [(codes == 2).astype(jnp.bfloat16), (codes == 1).astype(jnp.bfloat16)]
        ind = jnp.concatenate(ind, axis=0)
        for y in range(SIDE):
            table = []
            for j in range(len(ks)):
                u = w_ref[j] * ey_ref[j, y:y + 1, :]
                log_all = jnp.log(1.0 + u)
                table += [(jnp.log(guess[j] + u) - log_all).astype(jnp.bfloat16),
                          (log_rest[j] - log_all).astype(jnp.bfloat16)]
            ll_ref[0, y * rows_y:(y + 1) * rows_y, :] += jnp.dot(
                jnp.concatenate(table, axis=1), ind, preferred_element_type=jnp.float32)

    each_pair(count_ref[b], tiles)

    row_max = jnp.max(ll_ref[0], axis=0, keepdims=True)
    zero = jnp.zeros((rows_y, lanes), jnp.float32)

    def weigh(y, carry):
        total, by_y = carry
        w = jnp.exp(ll_ref[0, pl.ds(pl.multiple_of(y * rows_y, rows_y), rows_y), :] - row_max)
        th1 = lattice_point(jnp.full((1, lanes), y, jnp.int32))
        return total + w, by_y + w * th1

    total, by_y = lax.fori_loop(0, SIDE, weigh, (zero, zero), unroll=4)
    sums = [total, total * th0, by_y, total * th2]
    red_ref[0] = jnp.concatenate(
        [row_max] + [jnp.sum(s, axis=0, keepdims=True) for s in sums] + [jnp.zeros((3, lanes), jnp.float32)], axis=0)


def stats_kernel(planes, items_ref, count_ref, x0_ref, resp_ref, tab_ref, ll_ref, norm_ref, out_ref, marg_ref, mean_ref, ey_ref, w_ref, post_ref):
    b = pl.program_id(0)
    x0 = x0_ref[0]
    rows_y = planes * SIDE
    lanes = resp_ref.shape[-1]

    @pl.when(b == 0)
    def _():
        out_ref[...] = jnp.zeros_like(out_ref)

    log_norm = norm_ref[0, 0:1, :]
    marg_ref[...] = log_norm
    mean_ref[...] = norm_ref[0, 1:4, :]
    post_ref[...] = jnp.exp(ll_ref[0] - log_norm).astype(jnp.bfloat16)
    th2 = lattice_point(row_index((SIDE, lanes)))

    low = -3.0 + STEP * x0.astype(jnp.float32)
    zero = jnp.zeros((SIDE, lanes), jnp.float32)

    def chunk(post, ind, guess, e1, w):
        both = jnp.dot(post, ind, preferred_element_type=jnp.float32)
        s0 = s1 = f0 = f1 = f2 = zero
        for x in reversed(range(planes)):
            lo, hi = x * SIDE, (x + 1) * SIDE
            hits, mass = both[lo:hi, :lanes], both[lo:hi, lanes:]
            u = w[lo:hi, :] * e1
            cu, u1 = guess + u, 1.0 + u
            under = cu * u1
            first = pl.reciprocal(under, approx=True)
            uk = (u * first) * (2.0 - under * first)
            mc = mass * cu
            s0 = s0 + (hits * u1 - mc) * uk
            f0 = f0 + mc * (uk * uk)
            if x > 0:
                s1, f1 = s1 + s0, f1 + f0
                f2 = f2 + f1
        sx = low * s0 + STEP * s1
        fx = (low * low) * f0 + (2.0 * STEP * low - STEP * STEP) * f1 + (2.0 * STEP * STEP) * f2
        return s0, sx, f0, fx

    def tiles(ks):
        guess, ind, sums = [], [], []
        for j, k in enumerate(ks):
            rows = item_rows(tab_ref, items_ref[b, k])
            exp_factors(rows, x0, planes, ey_ref.at[j], w_ref.at[j])
            guess.append(rows[4])
            codes = resp_ref[0, k]
            ind.append(jnp.concatenate(
                [(codes == 2).astype(jnp.bfloat16), (codes > 0).astype(jnp.bfloat16)], axis=1))
            sums.append((zero,) * 6)
        for y in range(SIDE):
            th1 = -3.0 + STEP * y
            post = post_ref[y * rows_y:(y + 1) * rows_y, :]
            for j in range(len(ks)):
                s0, sx, f0, fx = chunk(post, ind[j], guess[j], ey_ref[j, y:y + 1, :], w_ref.at[j])
                g, gy, gx, h, hy, hx = sums[j]
                sums[j] = (g + s0, gy + s0 * th1, gx + sx, h + f0, hy + f0 * (th1 * th1), hx + fx)
        for j, k in enumerate(ks):
            g, gy, gx, h, hy, hx = sums[j]
            score_sums = [jnp.sum(v, axis=0, keepdims=True) for v in (gx, gy, g * th2, g)]
            fisher_sums = [(1.0 - guess[j]) * jnp.sum(v, axis=0, keepdims=True)
                           for v in (hx, hy, h * (th2 * th2), h)]
            out_ref[items_ref[b, k]] += jnp.concatenate(score_sums + fisher_sums, axis=0)

    each_pair(count_ref[b], tiles)


def enter(me, takers, core):
    barrier = pltpu.get_barrier_semaphore()

    def greet(o, carry):
        pl.semaphore_signal(barrier, inc=1, device_id=(lax.rem(me + o, takers), core), device_id_type=MESH)
        return carry

    lax.fori_loop(1, takers, greet, 0)
    pl.semaphore_signal(barrier, inc=1, device_id=(me, 1 - core), device_id_type=MESH)
    pl.semaphore_wait(barrier, takers)


def gather_kernel(takers, slope_ref, icpt_ref, guess_ref, tab_ref, mine_ref, held, send1, recv1, send2, recv2):
    me, core = lax.axis_index("takers"), lax.axis_index("nodes")
    rows = mine_ref.shape[0]
    half = rows // 2
    own = rows // 5
    here = pl.ds(pl.multiple_of(core * half, half), half)
    lanes = mine_ref.shape[1]
    for p in range(3):
        line = slope_ref[p:p + 1, :].astype(jnp.float32)
        mine_ref[p * own:(p + 1) * own, :] = jnp.concatenate(
            [line[:, i * lanes:(i + 1) * lanes] for i in range(own)], axis=0).astype(jnp.bfloat16)
    mine_ref[3 * own:4 * own, :] = icpt_ref[...]
    mine_ref[4 * own:, :] = guess_ref[...]
    enter(me, takers, core)

    def away(o):
        return pltpu.make_async_remote_copy(
            src_ref=mine_ref.at[here, :], dst_ref=held.at[me, here, :], send_sem=send1.at[o], recv_sem=recv1.at[o],
            device_id=(lax.rem(me + o, takers), core), device_id_type=MESH)

    def across(o):
        part = held.at[lax.rem(me + takers - o, takers), here, :]
        return pltpu.make_async_remote_copy(
            src_ref=part, dst_ref=part, send_sem=send2.at[o], recv_sem=recv2.at[o],
            device_id=(me, 1 - core), device_id_type=MESH)

    def spread(source, value):
        for p in range(5):
            tab_ref[p, pl.ds(pl.multiple_of(source * own, own), own), :] = value[p * own:(p + 1) * own].astype(jnp.float32)

    def begin(o, carry):
        away(o).start()
        return carry

    def forward(o, carry):
        away(o).wait_recv()
        across(o).start()
        return carry

    def finish(o, carry):
        across(o).wait_recv()
        source = lax.rem(me + takers - o, takers)
        spread(source, held[source])
        return carry

    def drain(o, carry):
        away(o).wait_send()
        across(o).wait_send()
        return carry

    lax.fori_loop(1, takers, begin, 0)
    spread(me, mine_ref[...])
    lax.fori_loop(1, takers, forward, 0)
    lax.fori_loop(1, takers, finish, 0)
    lax.fori_loop(1, takers, drain, 0)


def combine_kernel(red_ref, out_ref, theirs, send, recv):
    me, core = lax.axis_index("takers"), lax.axis_index("nodes")
    barrier = pltpu.get_barrier_semaphore()
    pl.semaphore_signal(barrier, inc=1, device_id=(me, 1 - core), device_id_type=MESH)
    pl.semaphore_wait(barrier, 1)
    copy = pltpu.make_async_remote_copy(
        src_ref=red_ref, dst_ref=theirs, send_sem=send, recv_sem=recv, device_id=(me, 1 - core), device_id_type=MESH)
    copy.start()
    copy.wait()
    for b in range(red_ref.shape[0]):
        a, t = red_ref[b], theirs[b]
        top = jnp.maximum(a[0:1], t[0:1])
        sums = a[1:5] * jnp.exp(a[0:1] - top) + t[1:5] * jnp.exp(t[0:1] - top)
        log_norm = top + jnp.log(sums[0:1])
        out_ref[b] = jnp.concatenate([log_norm, sums[1:4] / sums[0:1], jnp.zeros_like(a[4:])], axis=0)


def reduce_kernel(takers, dense_ref, slope_ref, icpt_ref, out_ref, out1, in1, out2, in2, sum_out, sum_in, summed,
                  send1, recv1, send2, recv2, send3, recv3):
    me, core = lax.axis_index("takers"), lax.axis_index("nodes")
    half = out1.shape[1]

    def piece(owner, side):
        return pl.ds(pl.multiple_of((owner * 2 + side) * half, half), half)

    def across(o):
        owner = lax.rem(me + o, takers)
        return pltpu.make_async_remote_copy(
            src_ref=out1.at[owner], dst_ref=in1.at[owner], send_sem=send1.at[o], recv_sem=recv1.at[o],
            device_id=(me, 1 - core), device_id_type=MESH)

    def away(o):
        owner = lax.rem(me + o, takers)
        return pltpu.make_async_remote_copy(
            src_ref=out2.at[owner], dst_ref=in2.at[me], send_sem=send2.at[o], recv_sem=recv2.at[o],
            device_id=(owner, core), device_id_type=MESH)

    def both(owner):
        return dense_ref[piece(owner, core), :] + in1[owner].astype(jnp.float32)

    def begin(o, carry):
        owner = lax.rem(me + o, takers)
        out1[owner] = dense_ref[piece(owner, 1 - core), :].astype(jnp.bfloat16)
        across(o).start()
        return carry

    def forward(o, carry):
        owner = lax.rem(me + o, takers)
        across(o).wait_recv()
        out2[owner] = both(owner).astype(jnp.bfloat16)
        away(o).start()
        return carry

    def add(o, carry):
        away(o).wait_recv()
        sum_out[...] += in2[lax.rem(me + takers - o, takers)].astype(jnp.float32)
        return carry

    def drain(o, carry):
        across(o).wait_send()
        away(o).wait_send()
        return carry

    enter(me, takers, core)
    lax.fori_loop(1, takers, begin, 0)
    begin(0, 0)
    lax.fori_loop(1, takers, forward, 0)
    across(0).wait_recv()
    sum_out[...] = both(me)
    lax.fori_loop(1, takers, add, 0)
    last = pltpu.make_async_remote_copy(
        src_ref=sum_out, dst_ref=sum_in, send_sem=send3, recv_sem=recv3, device_id=(me, 1 - core), device_id_type=MESH)
    last.start()
    summed[pl.ds(pl.multiple_of(core * half, half), half), :] = sum_out[...]
    lax.fori_loop(1, takers, drain, 0)
    across(0).wait_send()
    last.wait()
    summed[pl.ds(pl.multiple_of((1 - core) * half, half), half), :] = sum_in[...]
    lanes = summed.shape[1]
    slope, icpt = slope_ref[...].astype(jnp.float32), icpt_ref[...].astype(jnp.float32)
    for i in range(2 * half // 8):
        here = slice(i * lanes, (i + 1) * lanes)
        now = jnp.concatenate([slope[:, here], icpt[i:i + 1]], axis=0)
        out_ref[:, here] = now + summed[8 * i:8 * i + 4, :] / (summed[8 * i + 4:8 * i + 8, :] + 1.0)


def remote_call(kernel, collective_id, out_shape, scratch, nbytes, *args):
    vmem = pl.BlockSpec(memory_space=pltpu.VMEM)
    return pl.pallas_call(
        kernel, out_shape=out_shape, in_specs=[vmem] * len(args), out_specs=vmem, scratch_shapes=scratch,
        compiler_params=pltpu.CompilerParams(
            collective_id=collective_id, has_side_effects=True, vmem_limit_bytes=VMEM_LIMIT),
        cost_estimate=pl.CostEstimate(flops=0, bytes_accessed=nbytes, transcendentals=0))(*args)


def paired(rows):
    return lax.axis_size("nodes") == 2 and rows % 32 == 0


def gather_params(slopes, intercepts, guessing, takers, lanes):
    blocks_own = intercepts.shape[0] // lanes
    rows = 5 * blocks_own
    if paired(rows) and blocks_own % 16 == 0:
        sems = [pltpu.SemaphoreType.DMA((takers,))] * 4
        return remote_call(
            functools.partial(gather_kernel, takers), 0,
            jax.ShapeDtypeStruct((5, takers * blocks_own, lanes), jnp.float32),
            [pltpu.VMEM((rows, lanes), jnp.bfloat16), pltpu.VMEM((takers, rows, lanes), jnp.bfloat16)] + sems, 4 << 20,
            slopes, intercepts.reshape(blocks_own, lanes),
            guessing.reshape(blocks_own, lanes))
    packed = jnp.concatenate([slopes, intercepts[None], guessing[None]], axis=0).reshape(rows, lanes)
    everyone = lax.all_gather(packed, "takers", axis=0, tiled=False)
    table = everyone.reshape(takers, 5, blocks_own, lanes)
    return jnp.transpose(table, (1, 0, 2, 3)).reshape(5, takers * blocks_own, lanes).astype(jnp.float32)


def combine_nodes(red):
    if lax.axis_size("nodes") == 2:
        return remote_call(
            combine_kernel, 1, jax.ShapeDtypeStruct(red.shape, jnp.float32),
            [pltpu.VMEM(red.shape, jnp.float32), pltpu.SemaphoreType.DMA, pltpu.SemaphoreType.DMA], 1 << 16, red)
    row_max = red[:, 0:1]
    top = lax.pmax(row_max, "nodes")
    sums = lax.psum(red[:, 1:5] * jnp.exp(row_max - top), "nodes")
    log_norm = top + jnp.log(sums[:, 0:1])
    return jnp.concatenate([log_norm, sums[:, 1:4] / sums[:, 0:1], jnp.zeros_like(red[:, 4:])], axis=1)


def update_items(dense, slopes, intercepts, takers):
    blocks, rows, lanes = dense.shape
    own = blocks // takers
    if paired(own * rows):
        half = own * rows // 2
        pieces = pltpu.VMEM((takers, half, lanes), jnp.bfloat16)
        total = pltpu.VMEM((half, lanes), jnp.float32)
        scratch = ([pieces] * 4 + [total] * 2 + [pltpu.VMEM((2 * half, lanes), jnp.float32)]
                   + [pltpu.SemaphoreType.DMA((takers,))] * 4 + [pltpu.SemaphoreType.DMA] * 2)
        return remote_call(
            functools.partial(reduce_kernel, takers), 2, jax.ShapeDtypeStruct((4, own * lanes), jnp.float32),
            scratch, 8 << 20, dense.reshape(blocks * rows, lanes), slopes, intercepts.reshape(own, lanes))
    summed = lax.psum(lax.psum_scatter(dense, "takers", scatter_dimension=0, tiled=True), "nodes")
    summed = jnp.transpose(summed, (1, 0, 2)).reshape(rows, own * lanes)
    current = jnp.concatenate([slopes.astype(jnp.float32), intercepts.astype(jnp.float32)[None]], axis=0)
    return current + summed[:4] / (summed[4:] + 1.0)


def local(slopes, intercepts, guessing, responses, tile_items, tile_count):
    rowblk, slots, tile, _ = responses.shape
    takers, parts = lax.axis_size("takers"), lax.axis_size("nodes")
    planes = SIDE // parts
    nodes_here = planes * SIDE * SIDE
    rows_y = planes * SIDE
    items_own = intercepts.shape[0]
    blocks_own = items_own // tile
    blocks = blocks_own * takers
    table = gather_params(slopes, intercepts, guessing, takers, tile)
    x0 = (lax.axis_index("nodes") * planes).astype(jnp.int32).reshape(1)

    resp_spec = pl.BlockSpec((1, slots, tile, tile), lambda b, *_: (b, 0, 0, 0))
    table_spec = pl.BlockSpec((5, blocks, tile), lambda b, *_: (0, 0, 0))
    ll_spec = pl.BlockSpec((1, nodes_here, tile), lambda b, *_: (b, 0, 0))
    row_spec = pl.BlockSpec((1, 8, tile), lambda b, *_: (b, 0, 0))
    factors = [pltpu.VMEM((2, SIDE, tile), jnp.float32), pltpu.VMEM((2, rows_y, tile), jnp.float32)]
    params = pltpu.CompilerParams(vmem_limit_bytes=VMEM_LIMIT, dimension_semantics=("arbitrary",))
    elements = rowblk * slots * tile * nodes_here

    loglik, red = pl.pallas_call(
        functools.partial(loglik_kernel, planes),
        grid_spec=pltpu.PrefetchScalarGridSpec(
            num_scalar_prefetch=3, grid=(rowblk,), in_specs=[resp_spec, table_spec],
            out_specs=[ll_spec, row_spec], scratch_shapes=factors),
        out_shape=[jax.ShapeDtypeStruct((rowblk, nodes_here, tile), jnp.float32),
                   jax.ShapeDtypeStruct((rowblk, 8, tile), jnp.float32)],
        compiler_params=params,
        cost_estimate=pl.CostEstimate(flops=elements * 512, bytes_accessed=10 << 20, transcendentals=2 * elements),
    )(tile_items, tile_count, x0, responses, table)

    norm_rows = combine_nodes(red)

    dense, marginal, posterior_mean = pl.pallas_call(
        functools.partial(stats_kernel, planes),
        grid_spec=pltpu.PrefetchScalarGridSpec(
            num_scalar_prefetch=3, grid=(rowblk,), in_specs=[resp_spec, table_spec, ll_spec, row_spec],
            out_specs=[pl.BlockSpec((blocks, 8, tile), lambda b, *_: (0, 0, 0)),
                       pl.BlockSpec((1, tile), lambda b, *_: (0, b)),
                       pl.BlockSpec((3, tile), lambda b, *_: (0, b))],
            scratch_shapes=factors + [pltpu.VMEM((nodes_here, tile), jnp.bfloat16)]),
        out_shape=[jax.ShapeDtypeStruct((blocks, 8, tile), jnp.float32),
                   jax.ShapeDtypeStruct((1, rowblk * tile), jnp.float32),
                   jax.ShapeDtypeStruct((3, rowblk * tile), jnp.float32)],
        compiler_params=params,
        cost_estimate=pl.CostEstimate(flops=elements * 512, bytes_accessed=12 << 20, transcendentals=elements),
    )(tile_items, tile_count, x0, responses, table, loglik, norm_rows)

    new_params = update_items(dense, slopes, intercepts, takers)
    return new_params, marginal.reshape(rowblk * tile), posterior_mean


def solution(mesh):
    in_specs = (
        P(None, "takers"),
        P("takers"),
        P("takers"),
        P("takers", None, None, None),
        P("takers", None),
        P("takers"),
    )
    out_specs = (P(None, "takers"), P("takers"), P(None, "takers"))
    return jax.shard_map(local, mesh=mesh, in_specs=in_specs, out_specs=out_specs, check_vma=False)
```

```python
import functools

import jax
import jax.numpy as jnp
from jax import lax
from jax.experimental import pallas as pl
from jax.experimental.pallas import tpu as pltpu
from jax.sharding import PartitionSpec as P

SIDE = 16
STEP = 6.0 / (SIDE - 1)
MESH = pl.DeviceIdType.MESH
GROUP = 4
VMEM_LIMIT = 56 * 1024 * 1024


def lattice_point(index):
    return -3.0 + 6.0 * index.astype(jnp.float32) / (SIDE - 1)


def item_rows(tab_ref, block):
    return [tab_ref[p, pl.ds(block, 1), :] for p in range(5)]


def each_pair(count, tiles):
    def pair(p, carry):
        tiles([2 * p, 2 * p + 1])
        return carry

    lax.fori_loop(0, count // 2, pair, 0)

    @pl.when(count % 2 == 1)
    def _():
        tiles([count - 1])


def exp_factors(rows, x0, planes, ey_ref, w_ref):
    a0, a1, a2, d, _ = rows
    line = lattice_point(lax.broadcasted_iota(jnp.int32, (SIDE, a0.shape[1]), 0))
    ey_ref[...] = jnp.exp(a1 * line)
    ez = jnp.exp(a2 * line + d)
    ex = jnp.exp(a0 * lattice_point(x0 + lax.broadcasted_iota(jnp.int32, (SIDE, a0.shape[1]), 0)))
    for x in range(planes):
        w_ref[x * SIDE:(x + 1) * SIDE, :] = ez * ex[x:x + 1, :]


def row_index(shape):
    return lax.broadcasted_iota(jnp.int32, shape, 0)


def loglik_kernel(planes, items_ref, count_ref, x0_ref, resp_ref, tab_ref, ll_ref, red_ref, ey_ref, w_ref):
    b = pl.program_id(0)
    x0 = x0_ref[0]
    rows_y = planes * SIDE
    lanes = resp_ref.shape[-1]
    line = lattice_point(row_index((SIDE, lanes)))
    log_total = 3.0 * jnp.log(jnp.sum(jnp.exp(-0.5 * line * line), axis=0, keepdims=True))
    within = row_index((rows_y, lanes))
    th0 = lattice_point(x0 + within // SIDE)
    th2 = lattice_point(within % SIDE)
    prior_xz = -0.5 * (th0 * th0 + th2 * th2) - log_total

    def init(y, carry):
        th1 = lattice_point(jnp.full((1, lanes), y, jnp.int32))
        ll_ref[0, pl.ds(pl.multiple_of(y * rows_y, rows_y), rows_y), :] = prior_xz - 0.5 * th1 * th1
        return carry

    lax.fori_loop(0, SIDE, init, 0, unroll=4)

    def tiles(ks):
        guess, log_rest, ind = [], [], []
        for j, k in enumerate(ks):
            rows = item_rows(tab_ref, items_ref[b, k])
            exp_factors(rows, x0, planes, ey_ref.at[j], w_ref.at[j])
            guess.append(rows[4])
            log_rest.append(jnp.log(1.0 - rows[4]))
            codes = resp_ref[0, k].T
            ind += [(codes == 2).astype(jnp.bfloat16), (codes == 1).astype(jnp.bfloat16)]
        ind = jnp.concatenate(ind, axis=0)
        for y0 in range(0, SIDE, GROUP):
            lines = []
            for y in range(y0, y0 + GROUP):
                table = []
                for j in range(len(ks)):
                    u = w_ref[j] * ey_ref[j, y:y + 1, :]
                    log_all = jnp.log(1.0 + u)
                    table += [(jnp.log(guess[j] + u) - log_all).astype(jnp.bfloat16),
                              (log_rest[j] - log_all).astype(jnp.bfloat16)]
                lines.append(jnp.concatenate(table, axis=1))
            ll_ref[0, y0 * rows_y:(y0 + GROUP) * rows_y, :] += jnp.dot(
                jnp.concatenate(lines, axis=0), ind, preferred_element_type=jnp.float32)

    each_pair(count_ref[b], tiles)

    row_max = jnp.max(ll_ref[0], axis=0, keepdims=True)
    zero = jnp.zeros((rows_y, lanes), jnp.float32)

    def weigh(y, carry):
        total, by_y = carry
        w = jnp.exp(ll_ref[0, pl.ds(pl.multiple_of(y * rows_y, rows_y), rows_y), :] - row_max)
        th1 = lattice_point(jnp.full((1, lanes), y, jnp.int32))
        return total + w, by_y + w * th1

    total, by_y = lax.fori_loop(0, SIDE, weigh, (zero, zero), unroll=4)
    sums = [total, total * th0, by_y, total * th2]
    red_ref[0] = jnp.concatenate(
        [row_max] + [jnp.sum(s, axis=0, keepdims=True) for s in sums] + [jnp.zeros((3, lanes), jnp.float32)], axis=0)


def stats_kernel(planes, items_ref, count_ref, x0_ref, resp_ref, tab_ref, ll_ref, norm_ref, out_ref, marg_ref, mean_ref, ey_ref, w_ref, post_ref):
    b = pl.program_id(0)
    x0 = x0_ref[0]
    rows_y = planes * SIDE
    lanes = resp_ref.shape[-1]

    @pl.when(b == 0)
    def _():
        out_ref[...] = jnp.zeros_like(out_ref)

    log_norm = norm_ref[0, 0:1, :]
    marg_ref[...] = log_norm
    mean_ref[...] = norm_ref[0, 1:4, :]
    post_ref[...] = jnp.exp(ll_ref[0] - log_norm).astype(jnp.bfloat16)
    th2 = lattice_point(row_index((SIDE, lanes)))

    low = -3.0 + STEP * x0.astype(jnp.float32)
    zero = jnp.zeros((SIDE, lanes), jnp.float32)

    def chunk(both, guess, e1, w):
        s0 = s1 = f0 = f1 = f2 = zero
        for x in reversed(range(planes)):
            lo, hi = x * SIDE, (x + 1) * SIDE
            hits, mass = both[lo:hi, :lanes], both[lo:hi, lanes:]
            u = w[lo:hi, :] * e1
            cu, u1 = guess + u, 1.0 + u
            under = cu * u1
            first = pl.reciprocal(under, approx=True)
            uk = (u * first) * (2.0 - under * first)
            mc = mass * cu
            s0 = s0 + (hits * u1 - mc) * uk
            f0 = f0 + mc * (uk * uk)
            if x > 0:
                s1, f1 = s1 + s0, f1 + f0
                f2 = f2 + f1
        sx = low * s0 + STEP * s1
        fx = (low * low) * f0 + (2.0 * STEP * low - STEP * STEP) * f1 + (2.0 * STEP * STEP) * f2
        return s0, sx, f0, fx

    def tiles(ks):
        guess, ind, sums = [], [], []
        for j, k in enumerate(ks):
            rows = item_rows(tab_ref, items_ref[b, k])
            exp_factors(rows, x0, planes, ey_ref.at[j], w_ref.at[j])
            guess.append(rows[4])
            codes = resp_ref[0, k]
            ind.append(jnp.concatenate(
                [(codes == 2).astype(jnp.bfloat16), (codes > 0).astype(jnp.bfloat16)], axis=1))
            sums.append((zero,) * 6)
        for y0 in range(0, SIDE, GROUP):
            post = post_ref[y0 * rows_y:(y0 + GROUP) * rows_y, :]
            for j in range(len(ks)):
                both = jnp.dot(post, ind[j], preferred_element_type=jnp.float32)
                for y in range(y0, y0 + GROUP):
                    th1 = -3.0 + STEP * y
                    s0, sx, f0, fx = chunk(
                        both[(y - y0) * rows_y:(y - y0 + 1) * rows_y], guess[j], ey_ref[j, y:y + 1, :], w_ref.at[j])
                    g, gy, gx, h, hy, hx = sums[j]
                    sums[j] = (g + s0, gy + s0 * th1, gx + sx, h + f0, hy + f0 * (th1 * th1), hx + fx)
        for j, k in enumerate(ks):
            g, gy, gx, h, hy, hx = sums[j]
            score_sums = [jnp.sum(v, axis=0, keepdims=True) for v in (gx, gy, g * th2, g)]
            fisher_sums = [(1.0 - guess[j]) * jnp.sum(v, axis=0, keepdims=True)
                           for v in (hx, hy, h * (th2 * th2), h)]
            out_ref[items_ref[b, k]] += jnp.concatenate(score_sums + fisher_sums, axis=0)

    each_pair(count_ref[b], tiles)


def enter(me, takers, core):
    barrier = pltpu.get_barrier_semaphore()

    def greet(o, carry):
        pl.semaphore_signal(barrier, inc=1, device_id=(lax.rem(me + o, takers), core), device_id_type=MESH)
        return carry

    lax.fori_loop(1, takers, greet, 0)
    pl.semaphore_signal(barrier, inc=1, device_id=(me, 1 - core), device_id_type=MESH)
    pl.semaphore_wait(barrier, takers)


def gather_kernel(takers, slope_ref, icpt_ref, guess_ref, tab_ref, mine_ref, held, send1, recv1, send2, recv2):
    me, core = lax.axis_index("takers"), lax.axis_index("nodes")
    rows = mine_ref.shape[0]
    half = rows // 2
    own = rows // 5
    here = pl.ds(pl.multiple_of(core * half, half), half)
    lanes = mine_ref.shape[1]
    for p in range(3):
        line = slope_ref[p:p + 1, :].astype(jnp.float32)
        mine_ref[p * own:(p + 1) * own, :] = jnp.concatenate(
            [line[:, i * lanes:(i + 1) * lanes] for i in range(own)], axis=0).astype(jnp.bfloat16)
    mine_ref[3 * own:4 * own, :] = icpt_ref[...]
    mine_ref[4 * own:, :] = guess_ref[...]
    enter(me, takers, core)

    def away(o):
        return pltpu.make_async_remote_copy(
            src_ref=mine_ref.at[here, :], dst_ref=held.at[me, here, :], send_sem=send1.at[o], recv_sem=recv1.at[o],
            device_id=(lax.rem(me + o, takers), core), device_id_type=MESH)

    def across(o):
        part = held.at[lax.rem(me + takers - o, takers), here, :]
        return pltpu.make_async_remote_copy(
            src_ref=part, dst_ref=part, send_sem=send2.at[o], recv_sem=recv2.at[o],
            device_id=(me, 1 - core), device_id_type=MESH)

    def spread(source, value):
        for p in range(5):
            tab_ref[p, pl.ds(pl.multiple_of(source * own, own), own), :] = value[p * own:(p + 1) * own].astype(jnp.float32)

    def begin(o, carry):
        away(o).start()
        return carry

    def forward(o, carry):
        away(o).wait_recv()
        across(o).start()
        return carry

    def finish(o, carry):
        across(o).wait_recv()
        source = lax.rem(me + takers - o, takers)
        spread(source, held[source])
        return carry

    def drain(o, carry):
        away(o).wait_send()
        across(o).wait_send()
        return carry

    lax.fori_loop(1, takers, begin, 0)
    spread(me, mine_ref[...])
    lax.fori_loop(1, takers, forward, 0)
    lax.fori_loop(1, takers, finish, 0)
    lax.fori_loop(1, takers, drain, 0)


def combine_kernel(red_ref, out_ref, theirs, send, recv):
    me, core = lax.axis_index("takers"), lax.axis_index("nodes")
    barrier = pltpu.get_barrier_semaphore()
    pl.semaphore_signal(barrier, inc=1, device_id=(me, 1 - core), device_id_type=MESH)
    pl.semaphore_wait(barrier, 1)
    copy = pltpu.make_async_remote_copy(
        src_ref=red_ref, dst_ref=theirs, send_sem=send, recv_sem=recv, device_id=(me, 1 - core), device_id_type=MESH)
    copy.start()
    copy.wait()
    for b in range(red_ref.shape[0]):
        a, t = red_ref[b], theirs[b]
        top = jnp.maximum(a[0:1], t[0:1])
        sums = a[1:5] * jnp.exp(a[0:1] - top) + t[1:5] * jnp.exp(t[0:1] - top)
        log_norm = top + jnp.log(sums[0:1])
        out_ref[b] = jnp.concatenate([log_norm, sums[1:4] / sums[0:1], jnp.zeros_like(a[4:])], axis=0)


def reduce_kernel(takers, dense_ref, slope_ref, icpt_ref, out_ref, out1, in1, out2, in2, sum_out, sum_in, summed,
                  send1, recv1, send2, recv2, send3, recv3):
    me, core = lax.axis_index("takers"), lax.axis_index("nodes")
    half = out1.shape[1]

    def piece(owner, side):
        return pl.ds(pl.multiple_of((owner * 2 + side) * half, half), half)

    def across(o):
        owner = lax.rem(me + o, takers)
        return pltpu.make_async_remote_copy(
            src_ref=out1.at[owner], dst_ref=in1.at[owner], send_sem=send1.at[o], recv_sem=recv1.at[o],
            device_id=(me, 1 - core), device_id_type=MESH)

    def away(o):
        owner = lax.rem(me + o, takers)
        return pltpu.make_async_remote_copy(
            src_ref=out2.at[owner], dst_ref=in2.at[me], send_sem=send2.at[o], recv_sem=recv2.at[o],
            device_id=(owner, core), device_id_type=MESH)

    def both(owner):
        return dense_ref[piece(owner, core), :] + in1[owner].astype(jnp.float32)

    def begin(o, carry):
        owner = lax.rem(me + o, takers)
        out1[owner] = dense_ref[piece(owner, 1 - core), :].astype(jnp.bfloat16)
        across(o).start()
        return carry

    def forward(o, carry):
        owner = lax.rem(me + o, takers)
        across(o).wait_recv()
        out2[owner] = both(owner).astype(jnp.bfloat16)
        away(o).start()
        return carry

    def add(o, carry):
        away(o).wait_recv()
        sum_out[...] += in2[lax.rem(me + takers - o, takers)].astype(jnp.float32)
        return carry

    def drain(o, carry):
        across(o).wait_send()
        away(o).wait_send()
        return carry

    enter(me, takers, core)
    lax.fori_loop(1, takers, begin, 0)
    begin(0, 0)
    lax.fori_loop(1, takers, forward, 0)
    across(0).wait_recv()
    sum_out[...] = both(me)
    lax.fori_loop(1, takers, add, 0)
    last = pltpu.make_async_remote_copy(
        src_ref=sum_out, dst_ref=sum_in, send_sem=send3, recv_sem=recv3, device_id=(me, 1 - core), device_id_type=MESH)
    last.start()
    summed[pl.ds(pl.multiple_of(core * half, half), half), :] = sum_out[...]
    lax.fori_loop(1, takers, drain, 0)
    across(0).wait_send()
    last.wait()
    summed[pl.ds(pl.multiple_of((1 - core) * half, half), half), :] = sum_in[...]
    lanes = summed.shape[1]
    slope, icpt = slope_ref[...].astype(jnp.float32), icpt_ref[...].astype(jnp.float32)
    for i in range(2 * half // 8):
        here = slice(i * lanes, (i + 1) * lanes)
        now = jnp.concatenate([slope[:, here], icpt[i:i + 1]], axis=0)
        out_ref[:, here] = now + summed[8 * i:8 * i + 4, :] / (summed[8 * i + 4:8 * i + 8, :] + 1.0)


def remote_call(kernel, collective_id, out_shape, scratch, nbytes, *args):
    vmem = pl.BlockSpec(memory_space=pltpu.VMEM)
    return pl.pallas_call(
        kernel, out_shape=out_shape, in_specs=[vmem] * len(args), out_specs=vmem, scratch_shapes=scratch,
        compiler_params=pltpu.CompilerParams(
            collective_id=collective_id, has_side_effects=True, vmem_limit_bytes=VMEM_LIMIT),
        cost_estimate=pl.CostEstimate(flops=0, bytes_accessed=nbytes, transcendentals=0))(*args)


def paired(rows):
    return lax.axis_size("nodes") == 2 and rows % 32 == 0


def gather_params(slopes, intercepts, guessing, takers, lanes):
    blocks_own = intercepts.shape[0] // lanes
    rows = 5 * blocks_own
    if paired(rows) and blocks_own % 16 == 0:
        sems = [pltpu.SemaphoreType.DMA((takers,))] * 4
        return remote_call(
            functools.partial(gather_kernel, takers), 0,
            jax.ShapeDtypeStruct((5, takers * blocks_own, lanes), jnp.float32),
            [pltpu.VMEM((rows, lanes), jnp.bfloat16), pltpu.VMEM((takers, rows, lanes), jnp.bfloat16)] + sems, 4 << 20,
            slopes, intercepts.reshape(blocks_own, lanes),
            guessing.reshape(blocks_own, lanes))
    packed = jnp.concatenate([slopes, intercepts[None], guessing[None]], axis=0).reshape(rows, lanes)
    everyone = lax.all_gather(packed, "takers", axis=0, tiled=False)
    table = everyone.reshape(takers, 5, blocks_own, lanes)
    return jnp.transpose(table, (1, 0, 2, 3)).reshape(5, takers * blocks_own, lanes).astype(jnp.float32)


def combine_nodes(red):
    if lax.axis_size("nodes") == 2:
        return remote_call(
            combine_kernel, 1, jax.ShapeDtypeStruct(red.shape, jnp.float32),
            [pltpu.VMEM(red.shape, jnp.float32), pltpu.SemaphoreType.DMA, pltpu.SemaphoreType.DMA], 1 << 16, red)
    row_max = red[:, 0:1]
    top = lax.pmax(row_max, "nodes")
    sums = lax.psum(red[:, 1:5] * jnp.exp(row_max - top), "nodes")
    log_norm = top + jnp.log(sums[:, 0:1])
    return jnp.concatenate([log_norm, sums[:, 1:4] / sums[:, 0:1], jnp.zeros_like(red[:, 4:])], axis=1)


def update_items(dense, slopes, intercepts, takers):
    blocks, rows, lanes = dense.shape
    own = blocks // takers
    if paired(own * rows):
        half = own * rows // 2
        pieces = pltpu.VMEM((takers, half, lanes), jnp.bfloat16)
        total = pltpu.VMEM((half, lanes), jnp.float32)
        scratch = ([pieces] * 4 + [total] * 2 + [pltpu.VMEM((2 * half, lanes), jnp.float32)]
                   + [pltpu.SemaphoreType.DMA((takers,))] * 4 + [pltpu.SemaphoreType.DMA] * 2)
        return remote_call(
            functools.partial(reduce_kernel, takers), 2, jax.ShapeDtypeStruct((4, own * lanes), jnp.float32),
            scratch, 8 << 20, dense.reshape(blocks * rows, lanes), slopes, intercepts.reshape(own, lanes))
    summed = lax.psum(lax.psum_scatter(dense, "takers", scatter_dimension=0, tiled=True), "nodes")
    summed = jnp.transpose(summed, (1, 0, 2)).reshape(rows, own * lanes)
    current = jnp.concatenate([slopes.astype(jnp.float32), intercepts.astype(jnp.float32)[None]], axis=0)
    return current + summed[:4] / (summed[4:] + 1.0)


def local(slopes, intercepts, guessing, responses, tile_items, tile_count):
    rowblk, slots, tile, _ = responses.shape
    takers, parts = lax.axis_size("takers"), lax.axis_size("nodes")
    planes = SIDE // parts
    nodes_here = planes * SIDE * SIDE
    rows_y = planes * SIDE
    items_own = intercepts.shape[0]
    blocks_own = items_own // tile
    blocks = blocks_own * takers
    table = gather_params(slopes, intercepts, guessing, takers, tile)
    x0 = (lax.axis_index("nodes") * planes).astype(jnp.int32).reshape(1)

    resp_spec = pl.BlockSpec((1, slots, tile, tile), lambda b, *_: (b, 0, 0, 0))
    table_spec = pl.BlockSpec((5, blocks, tile), lambda b, *_: (0, 0, 0))
    ll_spec = pl.BlockSpec((1, nodes_here, tile), lambda b, *_: (b, 0, 0))
    row_spec = pl.BlockSpec((1, 8, tile), lambda b, *_: (b, 0, 0))
    factors = [pltpu.VMEM((2, SIDE, tile), jnp.float32), pltpu.VMEM((2, rows_y, tile), jnp.float32)]
    params = pltpu.CompilerParams(vmem_limit_bytes=VMEM_LIMIT, dimension_semantics=("arbitrary",))
    elements = rowblk * slots * tile * nodes_here

    loglik, red = pl.pallas_call(
        functools.partial(loglik_kernel, planes),
        grid_spec=pltpu.PrefetchScalarGridSpec(
            num_scalar_prefetch=3, grid=(rowblk,), in_specs=[resp_spec, table_spec],
            out_specs=[ll_spec, row_spec], scratch_shapes=factors),
        out_shape=[jax.ShapeDtypeStruct((rowblk, nodes_here, tile), jnp.float32),
                   jax.ShapeDtypeStruct((rowblk, 8, tile), jnp.float32)],
        compiler_params=params,
        cost_estimate=pl.CostEstimate(flops=elements * 512, bytes_accessed=10 << 20, transcendentals=2 * elements),
    )(tile_items, tile_count, x0, responses, table)

    norm_rows = combine_nodes(red)

    dense, marginal, posterior_mean = pl.pallas_call(
        functools.partial(stats_kernel, planes),
        grid_spec=pltpu.PrefetchScalarGridSpec(
            num_scalar_prefetch=3, grid=(rowblk,), in_specs=[resp_spec, table_spec, ll_spec, row_spec],
            out_specs=[pl.BlockSpec((blocks, 8, tile), lambda b, *_: (0, 0, 0)),
                       pl.BlockSpec((1, tile), lambda b, *_: (0, b)),
                       pl.BlockSpec((3, tile), lambda b, *_: (0, b))],
            scratch_shapes=factors + [pltpu.VMEM((nodes_here, tile), jnp.bfloat16)]),
        out_shape=[jax.ShapeDtypeStruct((blocks, 8, tile), jnp.float32),
                   jax.ShapeDtypeStruct((1, rowblk * tile), jnp.float32),
                   jax.ShapeDtypeStruct((3, rowblk * tile), jnp.float32)],
        compiler_params=params,
        cost_estimate=pl.CostEstimate(flops=elements * 512, bytes_accessed=12 << 20, transcendentals=elements),
    )(tile_items, tile_count, x0, responses, table, loglik, norm_rows)

    new_params = update_items(dense, slopes, intercepts, takers)
    return new_params, marginal.reshape(rowblk * tile), posterior_mean


def solution(mesh):
    in_specs = (
        P(None, "takers"),
        P("takers"),
        P("takers"),
        P("takers", None, None, None),
        P("takers", None),
        P("takers"),
    )
    out_specs = (P(None, "takers"), P("takers"), P(None, "takers"))
    return jax.shard_map(local, mesh=mesh, in_specs=in_specs, out_specs=out_specs, check_vma=False)
```

```python
import functools

import jax
import jax.numpy as jnp
from jax import lax
from jax.experimental import pallas as pl
from jax.experimental.pallas import tpu as pltpu
from jax.sharding import PartitionSpec as P

SIDE = 16
STEP = 6.0 / (SIDE - 1)
MESH = pl.DeviceIdType.MESH
PLANE = 4
GROUP = 4
VMEM_LIMIT = 56 * 1024 * 1024


def lattice_point(index):
    return -3.0 + 6.0 * index.astype(jnp.float32) / (SIDE - 1)


def item_rows(tab_ref, block):
    return [tab_ref[p, pl.ds(block, 1), :] for p in range(5)]


def each_pair(count, tiles):
    def pair(p, carry):
        tiles([2 * p, 2 * p + 1])
        return carry

    lax.fori_loop(0, count // 2, pair, 0)

    @pl.when(count % 2 == 1)
    def _():
        tiles([count - 1])


def exp_factors(rows, x0, planes, ey_ref, w_ref):
    a0, a1, a2, d, _ = rows
    line = lattice_point(lax.broadcasted_iota(jnp.int32, (SIDE, a0.shape[1]), 0))
    ey_ref[...] = jnp.exp(a1 * line)
    ez = jnp.exp(a2 * line + d)
    ex = jnp.exp(a0 * lattice_point(x0 + lax.broadcasted_iota(jnp.int32, (SIDE, a0.shape[1]), 0)))
    for x in range(planes):
        w_ref[x * SIDE:(x + 1) * SIDE, :] = ez * ex[x:x + 1, :]


def row_index(shape):
    return lax.broadcasted_iota(jnp.int32, shape, 0)


def loglik_kernel(planes, items_ref, count_ref, x0_ref, resp_ref, tab_ref, ll_ref, red_ref, ey_ref, w_ref):
    b = pl.program_id(0)
    x0 = x0_ref[0]
    rows_y = planes * SIDE
    lanes = resp_ref.shape[-1]
    line = lattice_point(row_index((SIDE, lanes)))
    log_total = 3.0 * jnp.log(jnp.sum(jnp.exp(-0.5 * line * line), axis=0, keepdims=True))
    within = row_index((rows_y, lanes))
    th0 = lattice_point(x0 + within // SIDE)
    th2 = lattice_point(within % SIDE)
    prior_xz = -0.5 * (th0 * th0 + th2 * th2) - log_total

    def init(y, carry):
        th1 = lattice_point(jnp.full((1, lanes), y, jnp.int32))
        ll_ref[0, pl.ds(pl.multiple_of(y * rows_y, rows_y), rows_y), :] = prior_xz - 0.5 * th1 * th1
        return carry

    lax.fori_loop(0, SIDE, init, 0, unroll=4)

    def tiles(ks):
        guess, log_rest, ind = [], [], []
        for j, k in enumerate(ks):
            rows = item_rows(tab_ref, items_ref[b, k])
            exp_factors(rows, x0, planes, ey_ref.at[j], w_ref.at[j])
            guess.append(rows[4])
            log_rest.append(jnp.log(1.0 - rows[4]))
            codes = resp_ref[0, k].T
            ind += [(codes == 2).astype(jnp.bfloat16), (codes == 1).astype(jnp.bfloat16)]
        ind = jnp.concatenate(ind, axis=0)
        for y0 in range(0, SIDE, GROUP):
            lines = []
            for y in range(y0, y0 + GROUP):
                table = []
                for j in range(len(ks)):
                    u = w_ref[j] * ey_ref[j, y:y + 1, :]
                    log_all = jnp.log(1.0 + u)
                    table += [(jnp.log(guess[j] + u) - log_all).astype(jnp.bfloat16),
                              (log_rest[j] - log_all).astype(jnp.bfloat16)]
                lines.append(jnp.concatenate(table, axis=1))
            ll_ref[0, y0 * rows_y:(y0 + GROUP) * rows_y, :] += jnp.dot(
                jnp.concatenate(lines, axis=0), ind, preferred_element_type=jnp.float32)

    each_pair(count_ref[b], tiles)

    row_max = jnp.max(ll_ref[0], axis=0, keepdims=True)
    zero = jnp.zeros((rows_y, lanes), jnp.float32)

    def weigh(y, carry):
        total, by_y = carry
        w = jnp.exp(ll_ref[0, pl.ds(pl.multiple_of(y * rows_y, rows_y), rows_y), :] - row_max)
        th1 = lattice_point(jnp.full((1, lanes), y, jnp.int32))
        return total + w, by_y + w * th1

    total, by_y = lax.fori_loop(0, SIDE, weigh, (zero, zero), unroll=4)
    sums = [total, total * th0, by_y, total * th2]
    red_ref[0] = jnp.concatenate(
        [row_max] + [jnp.sum(s, axis=0, keepdims=True) for s in sums] + [jnp.zeros((3, lanes), jnp.float32)], axis=0)


def stats_kernel(planes, items_ref, count_ref, x0_ref, resp_ref, tab_ref, ll_ref, norm_ref, out_ref, marg_ref, mean_ref, ey_ref, w_ref, post_ref):
    b = pl.program_id(0)
    x0 = x0_ref[0]
    rows_y = planes * SIDE
    lanes = resp_ref.shape[-1]

    @pl.when(b == 0)
    def _():
        out_ref[...] = jnp.zeros_like(out_ref)

    log_norm = norm_ref[0, 0:1, :]
    marg_ref[...] = log_norm
    mean_ref[...] = norm_ref[0, 1:4, :]
    post_ref[...] = jnp.exp(ll_ref[0] - log_norm).astype(jnp.bfloat16)
    th2 = lattice_point(row_index((SIDE, lanes)))

    low = -3.0 + STEP * x0.astype(jnp.float32)
    zero = jnp.zeros((SIDE, lanes), jnp.float32)

    def chunk(both, guess, e1, w):
        s0 = s1 = f0 = f1 = f2 = zero
        for x in reversed(range(planes)):
            lo, hi = x * SIDE, (x + 1) * SIDE
            hits, mass = both[lo:hi, :lanes], both[lo:hi, lanes:]
            u = w[lo:hi, :] * e1
            cu, u1 = guess + u, 1.0 + u
            under = cu * u1
            uk = u * pl.reciprocal(under, approx=True)
            mc = mass * cu
            s0 = s0 + (hits * u1 - mc) * uk
            f0 = f0 + mc * (uk * uk)
            if x > 0:
                s1, f1 = s1 + s0, f1 + f0
                f2 = f2 + f1
        sx = low * s0 + STEP * s1
        fx = (low * low) * f0 + (2.0 * STEP * low - STEP * STEP) * f1 + (2.0 * STEP * STEP) * f2
        return s0, sx, f0, fx

    def tiles(ks):
        guess, ind, sums = [], [], []
        for j, k in enumerate(ks):
            rows = item_rows(tab_ref, items_ref[b, k])
            exp_factors(rows, x0, planes, ey_ref.at[j], w_ref.at[j])
            guess.append(rows[4])
            codes = resp_ref[0, k]
            ind.append(jnp.concatenate(
                [(codes == 2).astype(jnp.bfloat16), (codes > 0).astype(jnp.bfloat16)], axis=1))
            sums.append((zero,) * 6)
        for y0 in range(0, SIDE, GROUP):
            post = post_ref[y0 * rows_y:(y0 + GROUP) * rows_y, :]
            for j in range(len(ks)):
                both = jnp.dot(post, ind[j], preferred_element_type=jnp.float32)
                for y in range(y0, y0 + GROUP):
                    th1 = -3.0 + STEP * y
                    s0, sx, f0, fx = chunk(
                        both[(y - y0) * rows_y:(y - y0 + 1) * rows_y], guess[j], ey_ref[j, y:y + 1, :], w_ref.at[j])
                    g, gy, gx, h, hy, hx = sums[j]
                    sums[j] = (g + s0, gy + s0 * th1, gx + sx, h + f0, hy + f0 * (th1 * th1), hx + fx)
        for j, k in enumerate(ks):
            g, gy, gx, h, hy, hx = sums[j]
            score_sums = [jnp.sum(v, axis=0, keepdims=True) for v in (gx, gy, g * th2, g)]
            fisher_sums = [(1.0 - guess[j]) * jnp.sum(v, axis=0, keepdims=True)
                           for v in (hx, hy, h * (th2 * th2), h)]
            out_ref[items_ref[b, k]] += jnp.concatenate(score_sums + fisher_sums, axis=0)

    each_pair(count_ref[b], tiles)


def enter(me, takers, core):
    barrier = pltpu.get_barrier_semaphore()

    def greet(o, carry):
        pl.semaphore_signal(barrier, inc=1, device_id=(lax.rem(me + o, takers), core), device_id_type=MESH)
        return carry

    lax.fori_loop(1, takers, greet, 0)
    pl.semaphore_signal(barrier, inc=1, device_id=(me, 1 - core), device_id_type=MESH)
    pl.semaphore_wait(barrier, takers)


def gather_kernel(takers, slope_ref, icpt_ref, guess_ref, tab_ref, mine_ref, held, send1, recv1, send2, recv2):
    me, core = lax.axis_index("takers"), lax.axis_index("nodes")
    rows = mine_ref.shape[0]
    half = rows // 2
    own = rows // 5
    here = pl.ds(pl.multiple_of(core * half, half), half)
    lanes = mine_ref.shape[1]
    for p in range(3):
        line = slope_ref[p:p + 1, :].astype(jnp.float32)
        mine_ref[p * own:(p + 1) * own, :] = jnp.concatenate(
            [line[:, i * lanes:(i + 1) * lanes] for i in range(own)], axis=0).astype(jnp.bfloat16)
    mine_ref[3 * own:4 * own, :] = icpt_ref[...]
    mine_ref[4 * own:, :] = guess_ref[...]
    enter(me, takers, core)

    def away(o):
        return pltpu.make_async_remote_copy(
            src_ref=mine_ref.at[here, :], dst_ref=held.at[me, here, :], send_sem=send1.at[o], recv_sem=recv1.at[o],
            device_id=(lax.rem(me + o, takers), core), device_id_type=MESH)

    def across(o):
        part = held.at[lax.rem(me + takers - o, takers), here, :]
        return pltpu.make_async_remote_copy(
            src_ref=part, dst_ref=part, send_sem=send2.at[o], recv_sem=recv2.at[o],
            device_id=(me, 1 - core), device_id_type=MESH)

    def spread(source, value):
        for p in range(5):
            tab_ref[p, pl.ds(pl.multiple_of(source * own, own), own), :] = value[p * own:(p + 1) * own].astype(jnp.float32)

    def begin(o, carry):
        away(o).start()
        return carry

    def forward(o, carry):
        away(o).wait_recv()
        across(o).start()
        return carry

    def finish(o, carry):
        across(o).wait_recv()
        source = lax.rem(me + takers - o, takers)
        spread(source, held[source])
        return carry

    def drain(o, carry):
        away(o).wait_send()
        across(o).wait_send()
        return carry

    lax.fori_loop(1, takers, begin, 0)
    spread(me, mine_ref[...])
    lax.fori_loop(1, takers, forward, 0)
    lax.fori_loop(1, takers, finish, 0)
    lax.fori_loop(1, takers, drain, 0)


def combine_kernel(red_ref, out_ref, theirs, send, recv):
    me, core = lax.axis_index("takers"), lax.axis_index("nodes")
    barrier = pltpu.get_barrier_semaphore()
    pl.semaphore_signal(barrier, inc=1, device_id=(me, 1 - core), device_id_type=MESH)
    pl.semaphore_wait(barrier, 1)
    copy = pltpu.make_async_remote_copy(
        src_ref=red_ref, dst_ref=theirs, send_sem=send, recv_sem=recv, device_id=(me, 1 - core), device_id_type=MESH)
    copy.start()
    copy.wait()
    for b in range(red_ref.shape[0]):
        a, t = red_ref[b], theirs[b]
        top = jnp.maximum(a[0:1], t[0:1])
        sums = a[1:5] * jnp.exp(a[0:1] - top) + t[1:5] * jnp.exp(t[0:1] - top)
        log_norm = top + jnp.log(sums[0:1])
        out_ref[b] = jnp.concatenate([log_norm, sums[1:4] / sums[0:1], jnp.zeros_like(a[4:])], axis=0)


def reduce_kernel(takers, dense_ref, slope_ref, icpt_ref, out_ref, out1, in1, out2, in2, out3, in3,
                  sum_out, sum_in, summed, send1, recv1, send2, recv2, send4, recv4, send3, recv3):
    me, core = lax.axis_index("takers"), lax.axis_index("nodes")
    half = out1.shape[1]
    depth = takers // PLANE
    z, q = me // PLANE, lax.rem(me, PLANE)

    def mate(dq):
        return z * PLANE + lax.rem(q + dq, PLANE)

    def level(dz):
        return lax.rem(z + dz, depth) * PLANE + q

    def owner_of(i):
        return lax.rem(z + lax.rem(i, depth), depth) * PLANE + lax.rem(q + i // depth, PLANE)

    def piece(owner, side):
        return pl.ds(pl.multiple_of((owner * 2 + side) * half, half), half)

    def across(i):
        owner = owner_of(i)
        return pltpu.make_async_remote_copy(
            src_ref=out1.at[owner], dst_ref=in1.at[owner], send_sem=send1.at[i], recv_sem=recv1.at[i],
            device_id=(me, 1 - core), device_id_type=MESH)

    def within(i):
        return pltpu.make_async_remote_copy(
            src_ref=out2.at[i], dst_ref=in2.at[i], send_sem=send2.at[i], recv_sem=recv2.at[i],
            device_id=(mate(i // depth), core), device_id_type=MESH)

    def along(dz):
        return pltpu.make_async_remote_copy(
            src_ref=out3.at[dz], dst_ref=in3.at[dz], send_sem=send4.at[dz], recv_sem=recv4.at[dz],
            device_id=(level(dz), core), device_id_type=MESH)

    def both(i):
        owner = owner_of(i)
        across(i).wait_recv()
        return dense_ref[piece(owner, core), :] + in1[owner].astype(jnp.float32)

    def plane_sum(dz):
        total = both(dz)
        for dq in range(1, PLANE):
            within(dq * depth + dz).wait_recv()
            total = total + in2[dq * depth + dz].astype(jnp.float32)
        return total

    def begin(i, carry):
        owner = owner_of(i)
        out1[owner] = dense_ref[piece(owner, 1 - core), :].astype(jnp.bfloat16)
        across(i).start()
        return carry

    def forward(i, carry):
        out2[i] = both(i).astype(jnp.bfloat16)
        within(i).start()
        return carry

    def climb(dz, carry):
        out3[dz] = plane_sum(dz).astype(jnp.bfloat16)
        along(dz).start()
        return carry

    def add(dz, carry):
        along(dz).wait_recv()
        sum_out[...] += in3[dz].astype(jnp.float32)
        return carry

    def drain1(i, carry):
        across(i).wait_send()
        return carry

    def drain2(i, carry):
        within(i).wait_send()
        return carry

    def drain3(dz, carry):
        along(dz).wait_send()
        return carry

    barrier = pltpu.get_barrier_semaphore()
    for dq in range(1, PLANE):
        pl.semaphore_signal(barrier, inc=1, device_id=(mate(dq), core), device_id_type=MESH)
    for dz in range(1, depth):
        pl.semaphore_signal(barrier, inc=1, device_id=(level(dz), core), device_id_type=MESH)
    pl.semaphore_signal(barrier, inc=1, device_id=(me, 1 - core), device_id_type=MESH)
    pl.semaphore_wait(barrier, PLANE + depth - 1)

    lax.fori_loop(depth, takers, begin, 0)
    lax.fori_loop(0, depth, begin, 0)
    lax.fori_loop(depth, takers, forward, 0)
    lax.fori_loop(1, depth, climb, 0)
    sum_out[...] = plane_sum(0)
    lax.fori_loop(1, depth, add, 0)
    last = pltpu.make_async_remote_copy(
        src_ref=sum_out, dst_ref=sum_in, send_sem=send3, recv_sem=recv3, device_id=(me, 1 - core), device_id_type=MESH)
    last.start()
    summed[pl.ds(pl.multiple_of(core * half, half), half), :] = sum_out[...]
    lax.fori_loop(0, takers, drain1, 0)
    lax.fori_loop(depth, takers, drain2, 0)
    lax.fori_loop(1, depth, drain3, 0)
    last.wait()
    summed[pl.ds(pl.multiple_of((1 - core) * half, half), half), :] = sum_in[...]
    lanes = summed.shape[1]
    slope, icpt = slope_ref[...].astype(jnp.float32), icpt_ref[...].astype(jnp.float32)
    for i in range(2 * half // 8):
        here = slice(i * lanes, (i + 1) * lanes)
        now = jnp.concatenate([slope[:, here], icpt[i:i + 1]], axis=0)
        out_ref[:, here] = now + summed[8 * i:8 * i + 4, :] / (summed[8 * i + 4:8 * i + 8, :] + 1.0)


def remote_call(kernel, collective_id, out_shape, scratch, nbytes, *args):
    vmem = pl.BlockSpec(memory_space=pltpu.VMEM)
    return pl.pallas_call(
        kernel, out_shape=out_shape, in_specs=[vmem] * len(args), out_specs=vmem, scratch_shapes=scratch,
        compiler_params=pltpu.CompilerParams(
            collective_id=collective_id, has_side_effects=True, vmem_limit_bytes=VMEM_LIMIT),
        cost_estimate=pl.CostEstimate(flops=0, bytes_accessed=nbytes, transcendentals=0))(*args)


def paired(rows):
    return lax.axis_size("nodes") == 2 and rows % 32 == 0


def gather_params(slopes, intercepts, guessing, takers, lanes):
    blocks_own = intercepts.shape[0] // lanes
    rows = 5 * blocks_own
    if paired(rows) and blocks_own % 16 == 0:
        sems = [pltpu.SemaphoreType.DMA((takers,))] * 4
        return remote_call(
            functools.partial(gather_kernel, takers), 0,
            jax.ShapeDtypeStruct((5, takers * blocks_own, lanes), jnp.float32),
            [pltpu.VMEM((rows, lanes), jnp.bfloat16), pltpu.VMEM((takers, rows, lanes), jnp.bfloat16)] + sems, 4 << 20,
            slopes, intercepts.reshape(blocks_own, lanes),
            guessing.reshape(blocks_own, lanes))
    packed = jnp.concatenate([slopes, intercepts[None], guessing[None]], axis=0).reshape(rows, lanes)
    everyone = lax.all_gather(packed, "takers", axis=0, tiled=False)
    table = everyone.reshape(takers, 5, blocks_own, lanes)
    return jnp.transpose(table, (1, 0, 2, 3)).reshape(5, takers * blocks_own, lanes).astype(jnp.float32)


def combine_nodes(red):
    if lax.axis_size("nodes") == 2:
        return remote_call(
            combine_kernel, 1, jax.ShapeDtypeStruct(red.shape, jnp.float32),
            [pltpu.VMEM(red.shape, jnp.float32), pltpu.SemaphoreType.DMA, pltpu.SemaphoreType.DMA], 1 << 16, red)
    row_max = red[:, 0:1]
    top = lax.pmax(row_max, "nodes")
    sums = lax.psum(red[:, 1:5] * jnp.exp(row_max - top), "nodes")
    log_norm = top + jnp.log(sums[:, 0:1])
    return jnp.concatenate([log_norm, sums[:, 1:4] / sums[:, 0:1], jnp.zeros_like(red[:, 4:])], axis=1)


def update_items(dense, slopes, intercepts, takers):
    blocks, rows, lanes = dense.shape
    own = blocks // takers
    if paired(own * rows) and takers % PLANE == 0:
        half = own * rows // 2
        pieces = pltpu.VMEM((takers, half, lanes), jnp.bfloat16)
        total = pltpu.VMEM((half, lanes), jnp.float32)
        levels = pltpu.VMEM((takers // PLANE, half, lanes), jnp.bfloat16)
        scratch = ([pieces] * 4 + [levels] * 2 + [total] * 2 + [pltpu.VMEM((2 * half, lanes), jnp.float32)]
                   + [pltpu.SemaphoreType.DMA((takers,))] * 6 + [pltpu.SemaphoreType.DMA] * 2)
        return remote_call(
            functools.partial(reduce_kernel, takers), 2, jax.ShapeDtypeStruct((4, own * lanes), jnp.float32),
            scratch, 8 << 20, dense.reshape(blocks * rows, lanes), slopes, intercepts.reshape(own, lanes))
    summed = lax.psum(lax.psum_scatter(dense, "takers", scatter_dimension=0, tiled=True), "nodes")
    summed = jnp.transpose(summed, (1, 0, 2)).reshape(rows, own * lanes)
    current = jnp.concatenate([slopes.astype(jnp.float32), intercepts.astype(jnp.float32)[None]], axis=0)
    return current + summed[:4] / (summed[4:] + 1.0)


def local(slopes, intercepts, guessing, responses, tile_items, tile_count):
    rowblk, slots, tile, _ = responses.shape
    takers, parts = lax.axis_size("takers"), lax.axis_size("nodes")
    planes = SIDE // parts
    nodes_here = planes * SIDE * SIDE
    rows_y = planes * SIDE
    items_own = intercepts.shape[0]
    blocks_own = items_own // tile
    blocks = blocks_own * takers
    table = gather_params(slopes, intercepts, guessing, takers, tile)
    x0 = (lax.axis_index("nodes") * planes).astype(jnp.int32).reshape(1)

    resp_spec = pl.BlockSpec((1, slots, tile, tile), lambda b, *_: (b, 0, 0, 0))
    table_spec = pl.BlockSpec((5, blocks, tile), lambda b, *_: (0, 0, 0))
    ll_spec = pl.BlockSpec((1, nodes_here, tile), lambda b, *_: (b, 0, 0))
    row_spec = pl.BlockSpec((1, 8, tile), lambda b, *_: (b, 0, 0))
    factors = [pltpu.VMEM((2, SIDE, tile), jnp.float32), pltpu.VMEM((2, rows_y, tile), jnp.float32)]
    params = pltpu.CompilerParams(vmem_limit_bytes=VMEM_LIMIT, dimension_semantics=("arbitrary",))
    elements = rowblk * slots * tile * nodes_here

    loglik, red = pl.pallas_call(
        functools.partial(loglik_kernel, planes),
        grid_spec=pltpu.PrefetchScalarGridSpec(
            num_scalar_prefetch=3, grid=(rowblk,), in_specs=[resp_spec, table_spec],
            out_specs=[ll_spec, row_spec], scratch_shapes=factors),
        out_shape=[jax.ShapeDtypeStruct((rowblk, nodes_here, tile), jnp.float32),
                   jax.ShapeDtypeStruct((rowblk, 8, tile), jnp.float32)],
        compiler_params=params,
        cost_estimate=pl.CostEstimate(flops=elements * 512, bytes_accessed=10 << 20, transcendentals=2 * elements),
    )(tile_items, tile_count, x0, responses, table)

    norm_rows = combine_nodes(red)

    dense, marginal, posterior_mean = pl.pallas_call(
        functools.partial(stats_kernel, planes),
        grid_spec=pltpu.PrefetchScalarGridSpec(
            num_scalar_prefetch=3, grid=(rowblk,), in_specs=[resp_spec, table_spec, ll_spec, row_spec],
            out_specs=[pl.BlockSpec((blocks, 8, tile), lambda b, *_: (0, 0, 0)),
                       pl.BlockSpec((1, tile), lambda b, *_: (0, b)),
                       pl.BlockSpec((3, tile), lambda b, *_: (0, b))],
            scratch_shapes=factors + [pltpu.VMEM((nodes_here, tile), jnp.bfloat16)]),
        out_shape=[jax.ShapeDtypeStruct((blocks, 8, tile), jnp.float32),
                   jax.ShapeDtypeStruct((1, rowblk * tile), jnp.float32),
                   jax.ShapeDtypeStruct((3, rowblk * tile), jnp.float32)],
        compiler_params=params,
        cost_estimate=pl.CostEstimate(flops=elements * 512, bytes_accessed=12 << 20, transcendentals=elements),
    )(tile_items, tile_count, x0, responses, table, loglik, norm_rows)

    new_params = update_items(dense, slopes, intercepts, takers)
    return new_params, marginal.reshape(rowblk * tile), posterior_mean


def solution(mesh):
    in_specs = (
        P(None, "takers"),
        P("takers"),
        P("takers"),
        P("takers", None, None, None),
        P("takers", None),
        P("takers"),
    )
    out_specs = (P(None, "takers"), P("takers"), P(None, "takers"))
    return jax.shard_map(local, mesh=mesh, in_specs=in_specs, out_specs=out_specs, check_vma=False)
```
